128 devices in a mesh: curve: 32 (over x, z, core), sub: 4 (over y).
Axes of the slice: x: 4, y: 4, z: 4, core: 2. Of those that a mesh axis runs over, the one named last changes fastest.
Arguments:
- child_poles: bfloat16 [8, 64, 262144], P(None, None, ('curve', 'sub')), may hold values from -6 to 6
- m2m_ops: bfloat16 [8, 64, 64], replicated, may hold values from -0.25 to 0.25
- m2l_ops: bfloat16 [316, 64, 64], replicated, may hold values from -0.078125 to 0.078125
- near_partner: int32 [88, 262144], P(None, ('curve', 'sub')), may hold values from -1 to 2047, as said below
- near_op: int32 [88], replicated, may hold values from 0 to 315, as said below
- far_source: int32 [128, 128, 128], P(('curve', 'sub')), may hold values from -1 to 2047, as said below
- far_target: int32 [128, 128, 128], P(('curve', 'sub')), may hold values from -1 to 2047, as said below
- far_op: int32 [128], replicated, may hold values from 0 to 315, as said below
Outputs:
- child_locals: bfloat16 [8, 64, 262144], P(None, None, ('curve', 'sub'))
The draws below stay inside these ranges and needn't reach their ends.
Inputs may be any that keep to these rules, and one draw needn't show every extreme that they name: `near_partner`: -1 marks an empty slot; otherwise the index, among the 2048 boxes of the box's own device, of a box later on the curve. `near_op`: distinct operator indices. `far_op`: distinct operator indices. `far_source`: entry [d, q, c] is -1 exactly where far_target[d, q, c] is -1 (an empty slot), always where q = d; otherwise an index among the boxes of device d. The used slots of each [d, q] come first; for every d some q has all 128 slots used. `far_target`: entry [d, q, c] is -1 exactly where far_source[d, q, c] is -1; otherwise an index among the boxes of device q.
All inputs are finite; a program needn't handle non-finite values.
Results may differ from the reference program's by a relative error of at most 0.0065.
Values may be sent and summed in bfloat16 or wider, within the bound.
No kernel may reach another device: no remote copies, remote signals or barrier semaphores. Data moves between devices by JAX's collectives and lax.ppermute only.
A program may use at most 128 MiB of HBM per device.

```python
import jax
import jax.numpy as jnp
from jax import lax

RANK = 64
CHILD = 8
NOFF = 316
PAIRS = 88
BOX_DEV = 2048
CAP = 128
PEERS = 128
BOXES = 262144


def far_layout(key):
    keys = jax.random.split(key, 5)
    reach = 8
    heavy = jax.random.randint(keys[0], (PEERS,), 1, 5)
    rows = jnp.arange(PEERS, dtype=jnp.int32)
    apart = rows[None, :] - rows[:, None]
    nearby = apart != 0
    counts = jax.random.randint(keys[1], (PEERS, PEERS), CAP // 4, CAP + 1) * heavy[:, None] // 4
    counts = jnp.where(nearby, counts, 0)
    offset = jax.random.randint(keys[2], (PEERS,), 1, reach + 1)
    full = jnp.where(rows + offset < PEERS, rows + offset, rows - offset)
    counts = jnp.where(rows[None, :] == full[:, None], CAP, counts)
    slot = jnp.arange(CAP, dtype=jnp.int32)
    used = slot[None, None, :] < counts[:, :, None]
    margin = BOX_DEV // 4
    source_rim = jax.random.randint(keys[3], (PEERS, PEERS, CAP), 0, margin)
    target_rim = jax.random.randint(keys[4], (PEERS, PEERS, CAP), 0, margin)
    later = (apart > 0)[:, :, None]
    source = jnp.where(later, BOX_DEV - 1 - source_rim, source_rim)
    target = jnp.where(later, target_rim, BOX_DEV - 1 - target_rim)
    corner = (rows[None, :] == full[:, None])[:, :, None] & (slot == 0)[None, None, :]
    source = jnp.where(corner, BOX_DEV - 1, source)
    target = jnp.where(corner, BOX_DEV - 1, target)
    return (jnp.where(used, source, -1).astype(jnp.int32), jnp.where(used, target, -1).astype(jnp.int32))


def pick_ops(key, count):
    keys = jax.random.split(key, 2)
    inner = jax.random.permutation(keys[0], NOFF - 2) + 1
    chosen = jnp.concatenate([jnp.array([0, NOFF - 1], jnp.int32), inner[:count - 2].astype(jnp.int32)])
    return jax.random.permutation(keys[1], chosen).astype(jnp.int32)


def draw_far_source(key, part):
    shared = far_layout(key)
    return shared[0]


def draw_far_target(key, part):
    shared = far_layout(key)
    return shared[1]


def draw_near_op(key, part):
    key = jax.random.fold_in(key, 5)
    return pick_ops(key, PAIRS)


def draw_far_op(key, part):
    key = jax.random.fold_in(key, 7)
    return pick_ops(key, CAP)


def draw_near_partner(key, part):
    key = jax.random.fold_in(key, 3)
    keys = jax.random.split(key, 3)
    box = jnp.arange(BOXES, dtype=jnp.int32)
    within = box % BOX_DEV
    owner = box // BOX_DEV
    delta = jax.random.randint(keys[0], (PAIRS, BOXES), 1, BOX_DEV // 2 + 1)
    target = within[None, :] + delta
    level = jax.random.randint(keys[1], (PEERS,), 1, 4)
    keep = jax.random.randint(keys[2], (PAIRS, BOXES), 0, 3) < level[owner][None, :]
    slot = jnp.arange(PAIRS, dtype=jnp.int32)[:, None]
    corner = (slot == 0) & (within[None, :] == 0)
    target = jnp.where(corner, BOX_DEV - 1, target)
    keep = keep | corner
    return jnp.where(keep & (target < BOX_DEV), target, -1).astype(jnp.int32)


def block_scale(rng, shape, cuts, low, high):
    def one(axis_at, parts):
        draws = jax.random.uniform(jax.random.fold_in(jax.random.fold_in(rng, 6), axis_at), (parts,), jnp.float32, low / len(cuts), high / len(cuts))
        return jnp.repeat(jnp.exp(draws), shape[axis_at] // parts).reshape((-1,) + (1,) * (len(shape) - axis_at - 1))

    factor_of = one(*cuts[0])
    for cut in cuts[1:]:
        factor_of = factor_of * one(*cut)
    return factor_of


def centred(key, shape, deviation, bound, shards=(), kind=jnp.bfloat16):
    result = jax.random.normal(key, shape, jnp.float32) * deviation
    if len(shards) > 0:
        result = block_scale(key, shape, shards, -0.22, 0.18) * result
    return jnp.clip(result, min=-bound, max=bound).astype(kind)


def setup_inputs(seed: int = 0) -> dict:
    key_list = jax.random.split(jax.random.key(seed), 9)
    child_poles = centred(key_list[0], (CHILD, RANK, BOXES), 1.0, 6.0, ((2, 128),))
    m2m_ops = centred(key_list[1], (CHILD, RANK, RANK), (CHILD * RANK) ** -0.5, 0.25)
    m2l_ops = centred(key_list[2], (NOFF, RANK, RANK), (RANK * PAIRS) ** -0.5, 0.078125)
    near_partner = draw_near_partner(jax.random.fold_in(key_list[8], 71), 0)
    near_op = draw_near_op(jax.random.fold_in(key_list[8], 71), 0)
    far_source = draw_far_source(jax.random.fold_in(key_list[8], 71), 0)
    far_target = draw_far_target(jax.random.fold_in(key_list[8], 71), 0)
    far_op = draw_far_op(jax.random.fold_in(key_list[8], 71), 0)
    return {"child_poles": child_poles, "m2m_ops": m2m_ops, "m2l_ops": m2l_ops, "near_partner": near_partner, "near_op": near_op, "far_source": far_source, "far_target": far_target, "far_op": far_op}


def reference(child_poles, m2m_ops, m2l_ops, near_partner, near_op, far_source, far_target, far_op):
    wide = jnp.float32
    poles = jnp.einsum("cij,cjb->ib", m2m_ops.astype(wide), child_poles.astype(wide)).astype(jnp.bfloat16)
    poles_wide = poles.astype(wide)
    boxes = poles.shape[1]
    base = (jnp.arange(boxes, dtype=jnp.int32) // BOX_DEV) * BOX_DEV

    def near_step(local, slot):
        partner, op_index = slot
        valid = partner >= 0
        column = base + jnp.maximum(partner, 0).astype(jnp.int32)
        operator = m2l_ops[op_index].astype(wide)
        ahead = jnp.dot(operator, poles_wide[:, column])
        back = jnp.dot(operator.T, poles_wide)
        local = local + jnp.where(valid[None, :], ahead, 0.0)
        local = local.at[:, column].add(jnp.where(valid[None, :], back, 0.0))
        return local, None

    local, _ = lax.scan(near_step, jnp.zeros((RANK, boxes), wide), (near_partner, near_op))
    owners = jnp.arange(PEERS, dtype=jnp.int32) * BOX_DEV

    def far_step(local, slot):
        source, target, op_index = slot
        valid = (source >= 0).reshape(-1)
        first = (owners[:, None] + jnp.maximum(source, 0).astype(jnp.int32)).reshape(-1)
        second = (owners[None, :] + jnp.maximum(target, 0).astype(jnp.int32)).reshape(-1)
        operator = m2l_ops[op_index].astype(wide)
        ahead = jnp.dot(operator, poles_wide[:, second])
        back = jnp.dot(operator.T, poles_wide[:, first])
        local = local.at[:, first].add(jnp.where(valid[None, :], ahead, 0.0))
        local = local.at[:, second].add(jnp.where(valid[None, :], back, 0.0))
        return local, None

    local, _ = lax.scan(far_step, local, (jnp.transpose(far_source, (2, 0, 1)), jnp.transpose(far_target, (2, 0, 1)), far_op))
    rounded_local = local.astype(jnp.bfloat16)
    return jnp.einsum("cji,jb->cib", m2m_ops.astype(wide), rounded_local.astype(wide)).astype(jnp.bfloat16)
```

```python
import functools

import jax
import jax.numpy as jnp
from jax import lax
from jax.experimental import pallas as pl
from jax.experimental.pallas import tpu as pltpu
from jax.sharding import PartitionSpec as P

RANK = 64
CHILD = 8
BOX = 2048
PEERS = 128
CAP = 128
PAIRS = 88
GROUPS = 4
LANES = 128
WIDE = GROUPS * RANK
TB = 512
NB = BOX // TB
WIDTH = [(BOX - b * TB) // GROUPS for b in range(NB)]
START = [sum(WIDTH[:b]) for b in range(NB)]
BATCH = 4
SPAN = BOX // GROUPS
QUAD = 4
EMPTY = 512
CENTRE = 256
SENT = RANK + 16
f32 = jnp.float32
bf16 = jnp.bfloat16
VMEM = pl.BlockSpec(memory_space=pltpu.VMEM)
SMEM = pl.BlockSpec(memory_space=pltpu.SMEM)
LIMIT = 56 * 2**20
NT = (((1,), (1,)), ((), ()))
TN = (((0,), (0,)), ((), ()))


def fill_table(table_ref):
    table_ref[...] = (lax.broadcasted_iota(jnp.int32, table_ref.shape, 0) - CENTRE).astype(f32).astype(bf16)


def split_index(rel, valid, width):
    group = ((rel >= width).astype(jnp.int32) + (rel >= 2 * width).astype(jnp.int32)
             + (rel >= 3 * width).astype(jnp.int32))
    place = jnp.where(valid, rel - group * width - CENTRE, EMPTY)
    return place.astype(f32), jnp.where(valid, group, 0).astype(f32)


def one_hot(table_ref, place, rows):
    n = place.shape[1]
    row = jnp.broadcast_to(place, (16, n)).astype(bf16)
    parts = []
    for r in range(rows // 16):
        here = table_ref[r * 16:(r + 1) * 16, :]
        here = jnp.concatenate([here] * (n // LANES), axis=1)
        parts.append(jnp.where(here == row, jnp.ones((), bf16), jnp.zeros((), bf16)))
    return jnp.concatenate(parts, axis=0)


def pick_group(stacked, group):
    out = stacked[0:RANK]
    for k in range(1, GROUPS):
        out = jnp.where(group == float(k), stacked[k * RANK:(k + 1) * RANK], out)
    return out


def spread_group(values, group):
    n = values.shape[1]
    row = jnp.broadcast_to(group, (16, n)).astype(bf16)
    parts = []
    for k in range(GROUPS):
        mask = row == jnp.array(k, bf16)
        parts += [jnp.where(mask, values[r * 16:(r + 1) * 16], jnp.zeros((), bf16)) for r in range(RANK // 16)]
    return jnp.concatenate(parts, axis=0)


def stack_groups(poles_ref, stack_ref):
    for k in range(GROUPS):
        stack_ref[k * RANK:(k + 1) * RANK, :] = poles_ref[:, k * SPAN:(k + 1) * SPAN]


def gather_quads(table_ref, stack_ref, place_ref, group_ref, hot_ref, store):
    def quad(n, _):
        place = jnp.concatenate([place_ref[pl.ds(n * QUAD + i, 1), :] for i in range(QUAD)], axis=1)
        group = jnp.concatenate([group_ref[pl.ds(n * QUAD + i, 1), :] for i in range(QUAD)], axis=1)
        hot_ref[...] = one_hot(table_ref, place, SPAN)
        found = jnp.dot(stack_ref[...], hot_ref[...], preferred_element_type=f32)
        found = pick_group(found, group).astype(bf16)
        for i in range(QUAD):
            store(n * QUAD + i, found[:, i * CAP:(i + 1) * CAP])
        return 0

    lax.fori_loop(0, PEERS // QUAD, quad, 0)


def up_kernel(child_ref, m2m_ref, source_ref, target_ref, poles_ref, send_ref,
              table_ref, stack_ref, place_ref, group_ref, ask_place_ref, ask_group_ref, hot_ref):
    fill_table(table_ref)
    ops = jnp.concatenate([m2m_ref[c] for c in range(CHILD)], axis=1)
    for s in range(0, BOX, 512):
        poles_ref[:, s:s + 512] = jnp.dot(
            ops, child_ref[:, s:s + 512], preferred_element_type=f32).astype(bf16)
    stack_groups(poles_ref, stack_ref)
    source = source_ref[...]
    place_ref[...], group_ref[...] = split_index(source, source >= 0, SPAN)
    target = target_ref[...]
    ask_place_ref[...], ask_group_ref[...] = split_index(target, target >= 0, SPAN)
    sub = lax.broadcasted_iota(jnp.int32, (16, CAP), 0)

    def store(q, block):
        send_ref[q, 0:RANK, :] = block
        ask = jnp.where(sub == 0, ask_place_ref[pl.ds(q, 1), :],
                        jnp.where(sub == 1, ask_group_ref[pl.ds(q, 1), :], 0.0))
        send_ref[q, RANK:SENT, :] = ask.astype(bf16)

    gather_quads(table_ref, stack_ref, place_ref, group_ref, hot_ref, store)


def upward(child, m2m, source, target):
    return pl.pallas_call(
        up_kernel,
        out_shape=(jax.ShapeDtypeStruct((RANK, BOX), bf16), jax.ShapeDtypeStruct((PEERS, SENT, CAP), bf16)),
        in_specs=[VMEM] * 4,
        out_specs=(VMEM, VMEM),
        scratch_shapes=[
            pltpu.VMEM((SPAN, LANES), bf16),
            pltpu.VMEM((WIDE, SPAN), bf16),
            pltpu.VMEM((PEERS, CAP), f32),
            pltpu.VMEM((PEERS, CAP), f32),
            pltpu.VMEM((PEERS, CAP), f32),
            pltpu.VMEM((PEERS, CAP), f32),
            pltpu.VMEM((SPAN, QUAD * CAP), bf16),
        ],
        compiler_params=pltpu.CompilerParams(vmem_limit_bytes=LIMIT),
        cost_estimate=pl.CostEstimate(flops=10**10, bytes_accessed=6 << 20, transcendentals=0),
        name="upward",
    )(child, m2m, source, target)


def serve_kernel(poles_ref, received_ref, out_ref, table_ref, stack_ref, place_ref, group_ref, hot_ref):
    fill_table(table_ref)
    stack_groups(poles_ref, stack_ref)

    def unpack(d, _):
        ask = received_ref[d, RANK:SENT, :].astype(f32)
        place_ref[pl.ds(d, 1), :] = ask[0:1]
        group_ref[pl.ds(d, 1), :] = ask[1:2]
        return 0

    lax.fori_loop(0, PEERS, unpack, 0)

    def store(d, block):
        out_ref[d, :, :] = block

    gather_quads(table_ref, stack_ref, place_ref, group_ref, hot_ref, store)


def serve(poles, received):
    return pl.pallas_call(
        serve_kernel,
        out_shape=jax.ShapeDtypeStruct((PEERS, RANK, CAP), bf16),
        in_specs=[VMEM] * 2,
        out_specs=VMEM,
        scratch_shapes=[
            pltpu.VMEM((SPAN, LANES), bf16),
            pltpu.VMEM((WIDE, SPAN), bf16),
            pltpu.VMEM((PEERS, CAP), f32),
            pltpu.VMEM((PEERS, CAP), f32),
            pltpu.VMEM((SPAN, QUAD * CAP), bf16),
        ],
        compiler_params=pltpu.CompilerParams(vmem_limit_bytes=LIMIT),
        cost_estimate=pl.CostEstimate(flops=10**10, bytes_accessed=4 << 20, transcendentals=0),
        name="serve",
    )(poles, received)


def near_kernel(first, batches, op_ref, poles_ref, partner_ref, m2l_ref, out_ref,
                table_ref, stack_ref, place_ref, group_ref, back_ref, ahead_ref, hot_ref, *totals):
    fill_table(table_ref)
    for b in range(NB):
        for k in range(GROUPS):
            s = b * TB + k * WIDTH[b]
            stack_ref[k * RANK:(k + 1) * RANK, START[b]:START[b] + WIDTH[b]] = poles_ref[:, s:s + WIDTH[b]]
        totals[b][...] = jnp.zeros(totals[b].shape, f32)
    slots = batches * BATCH
    for r in range(0, slots, 8):
        n = min(8, slots - r)
        for b in range(NB):
            block = slice(b * TB, (b + 1) * TB)
            partner = partner_ref[first + r:first + r + n, block]
            place, group = split_index(partner - b * TB, partner >= 0, WIDTH[b])
            place_ref[r:r + n, block] = place
            group_ref[r:r + n, block] = group
    out_ref[...] = jnp.zeros(out_ref.shape, f32)

    def batch(n, _):
        ops = jnp.concatenate([m2l_ref[op_ref[first + n * BATCH + j]] for j in range(BATCH)], axis=1)
        back_ref[...] = lax.dot_general(ops, poles_ref[...], TN, preferred_element_type=f32).astype(bf16)
        for j in range(BATCH):
            rows = slice(j * RANK, (j + 1) * RANK)
            for b in range(NB):
                block = slice(b * TB, (b + 1) * TB)
                width = WIDTH[b]
                place = place_ref[pl.ds(n * BATCH + j, 1), block]
                group = group_ref[pl.ds(n * BATCH + j, 1), block]
                side = (j * NB + b) % 2
                hot_ref[side, :width, :] = one_hot(table_ref, place, width)
                hot = hot_ref[side, :width, :]
                found = jnp.dot(stack_ref[:, START[b]:START[b] + width], hot, preferred_element_type=f32)
                ahead_ref[rows, block] = pick_group(found, group).astype(bf16)
                spread = spread_group(back_ref[rows, block], group)
                totals[b][...] += lax.dot_general(hot, spread, NT, preferred_element_type=f32)
        out_ref[...] += jnp.dot(ops, ahead_ref[...], preferred_element_type=f32)
        return 0

    lax.fori_loop(0, batches, batch, 0)
    for b in range(NB):
        for k in range(GROUPS):
            s = b * TB + k * WIDTH[b]
            out_ref[:, s:s + WIDTH[b]] += jnp.transpose(totals[b][...][:, k * RANK:(k + 1) * RANK])


def near(near_op, poles, partner, m2l, first, batches):
    return pl.pallas_call(
        functools.partial(near_kernel, first, batches),
        out_shape=jax.ShapeDtypeStruct((RANK, BOX), f32),
        in_specs=[SMEM, VMEM, VMEM, VMEM],
        out_specs=VMEM,
        scratch_shapes=[
            pltpu.VMEM((LANES * 4, LANES), bf16),
            pltpu.VMEM((WIDE, sum(WIDTH)), bf16),
            pltpu.VMEM((batches * BATCH, BOX), f32),
            pltpu.VMEM((batches * BATCH, BOX), f32),
            pltpu.VMEM((BATCH * RANK, BOX), bf16),
            pltpu.VMEM((BATCH * RANK, BOX), bf16),
            pltpu.VMEM((2, WIDTH[0], TB), bf16),
        ] + [pltpu.VMEM((WIDTH[b], WIDE), f32) for b in range(NB)],
        compiler_params=pltpu.CompilerParams(vmem_limit_bytes=LIMIT),
        cost_estimate=pl.CostEstimate(flops=10**9 * batches * BATCH, bytes_accessed=6 << 20, transcendentals=0),
        name="near",
    )(near_op, poles, partner, m2l)


def down_kernel(op_ref, near_a_ref, near_b_ref, served_ref, own_ref, source_ref, m2l_ref, m2m_ref, out_ref,
                table_ref, place_ref, group_ref, hot_ref, spread_ref, total_ref, local_ref):
    fill_table(table_ref)
    source = source_ref[...]
    place, group = split_index(source, source >= 0, SPAN)
    place_ref[...] = jnp.transpose(place)
    group_ref[...] = jnp.transpose(group)
    total_ref[...] = jnp.zeros(total_ref.shape, f32)

    def quad(n, _):
        for side in range(2):
            values, places, groups = [], [], []
            for i in range(QUAD):
                c = n * QUAD + i
                op = m2l_ref[op_ref[c]]
                if side == 0:
                    value = jnp.dot(op, served_ref[c], preferred_element_type=f32)
                    places.append(place_ref[pl.ds(c, 1), :])
                    groups.append(group_ref[pl.ds(c, 1), :])
                else:
                    value = lax.dot_general(op, own_ref[c, 0:RANK, :], TN, preferred_element_type=f32)
                    ask = own_ref[c, RANK:SENT, :].astype(f32)
                    places.append(ask[0:1])
                    groups.append(ask[1:2])
                values.append(value.astype(bf16))
            lanes = slice(side * QUAD * PEERS, (side + 1) * QUAD * PEERS)
            hot_ref[:, lanes] = one_hot(table_ref, jnp.concatenate(places, axis=1), SPAN)
            spread_ref[:, lanes] = spread_group(jnp.concatenate(values, axis=1), jnp.concatenate(groups, axis=1))
        total_ref[...] += lax.dot_general(hot_ref[...], spread_ref[...], NT, preferred_element_type=f32)
        return 0

    lax.fori_loop(0, CAP // QUAD, quad, 0)
    for k in range(GROUPS):
        cols = slice(k * SPAN, (k + 1) * SPAN)
        far = jnp.transpose(total_ref[...][:, k * RANK:(k + 1) * RANK])
        local_ref[:, cols] = (near_a_ref[:, cols] + near_b_ref[:, cols] + far).astype(bf16)
    ops = jnp.concatenate([m2m_ref[c] for c in range(CHILD)], axis=1)
    for s in range(0, BOX, 256):
        out_ref[:, s:s + 256] = lax.dot_general(
            ops, local_ref[:, s:s + 256], TN, preferred_element_type=f32).astype(bf16)


def downward(far_op, near_a, near_b, served, own, source, m2l, m2m):
    return pl.pallas_call(
        down_kernel,
        out_shape=jax.ShapeDtypeStruct((CHILD * RANK, BOX), bf16),
        in_specs=[SMEM] + [VMEM] * 7,
        out_specs=VMEM,
        scratch_shapes=[
            pltpu.VMEM((SPAN, LANES), bf16),
            pltpu.VMEM((CAP, PEERS), f32),
            pltpu.VMEM((CAP, PEERS), f32),
            pltpu.VMEM((SPAN, 2 * QUAD * PEERS), bf16),
            pltpu.VMEM((WIDE, 2 * QUAD * PEERS), bf16),
            pltpu.VMEM((SPAN, WIDE), f32),
            pltpu.VMEM((RANK, BOX), bf16),
        ],
        compiler_params=pltpu.CompilerParams(vmem_limit_bytes=LIMIT),
        cost_estimate=pl.CostEstimate(flops=2 * 10**10, bytes_accessed=16 << 20, transcendentals=0),
        name="downward",
    )(far_op, near_a, near_b, served, own, source, m2l, m2m)


def on_device(child_poles, m2m_ops, m2l_ops, near_partner, near_op, far_source, far_target, far_op):
    child = child_poles.reshape(CHILD * RANK, BOX)
    source = far_source[0]
    poles, send = upward(child, m2m_ops, source, far_target[0])
    received = lax.all_to_all(send, ("curve", "sub"), split_axis=0, concat_axis=0, tiled=True)
    half = PAIRS // BATCH // 2
    near_a = near(near_op, poles, near_partner, m2l_ops, 0, half)
    answer = serve(poles, received)
    fetched = lax.all_to_all(answer, ("curve", "sub"), split_axis=0, concat_axis=0, tiled=True)
    near_b = near(near_op, poles, near_partner, m2l_ops, half * BATCH, PAIRS // BATCH - half)
    own = jnp.transpose(received, (2, 1, 0))
    served = jnp.transpose(fetched, (2, 1, 0))
    out = downward(far_op, near_a, near_b, served, own, source, m2l_ops, m2m_ops)
    return out.reshape(CHILD, RANK, BOX)


def solution(mesh):
    placed = (
        P(None, None, ("curve", "sub")),
        P(),
        P(),
        P(None, ("curve", "sub")),
        P(),
        P(("curve", "sub"), None, None),
        P(("curve", "sub"), None, None),
        P(),
    )
    return jax.shard_map(
        on_device,
        mesh=mesh,
        in_specs=placed,
        out_specs=P(None, None, ("curve", "sub")),
        check_vma=False,
    )
```

```python
import functools

import jax
import jax.numpy as jnp
from jax import lax
from jax.experimental import pallas as pl
from jax.experimental.pallas import tpu as pltpu
from jax.sharding import PartitionSpec as P

RANK = 64
CHILD = 8
BOX = 2048
PEERS = 128
CAP = 128
PAIRS = 88
LANES = 128
TB = 256
NB = BOX // TB
STACK = NB * RANK
BATCH = 4
WIDE = BATCH * RANK
SIDES = 4
FAR = 8
EMPTY = 512
SENT = RANK + 16
f32 = jnp.float32
bf16 = jnp.bfloat16
VMEM = pl.BlockSpec(memory_space=pltpu.VMEM)
LIMIT = 56 * 2**20
NT = (((1,), (1,)), ((), ()))
TN = (((0,), (0,)), ((), ()))


def fill_table(table_ref):
    table_ref[...] = lax.broadcasted_iota(jnp.int32, table_ref.shape, 0).astype(f32).astype(bf16)


def split_index(index):
    group = index >> 8
    place = jnp.where(index >= 0, index - group * TB, EMPTY)
    return place.astype(f32), jnp.maximum(group, 0).astype(f32)


def one_hot(table_ref, place):
    n = place.shape[1]
    row = jnp.broadcast_to(place, (16, n)).astype(bf16)
    parts = []
    for r in range(TB // 16):
        here = table_ref[r * 16:(r + 1) * 16, :]
        here = jnp.concatenate([here] * (n // LANES), axis=1)
        parts.append(jnp.where(here == row, jnp.ones((), bf16), jnp.zeros((), bf16)))
    return jnp.concatenate(parts, axis=0)


def pick_group(stacked, group, low=0):
    out = stacked[0:RANK]
    for k in range(low + 1, NB):
        out = jnp.where(group == float(k), stacked[(k - low) * RANK:(k - low + 1) * RANK], out)
    return out


def spread_group(values, group, low=0):
    n = values.shape[1]
    row = jnp.broadcast_to(group, (16, n)).astype(bf16)
    parts = []
    for k in range(low, NB):
        mask = row == jnp.array(k, bf16)
        parts += [jnp.where(mask, values[r * 16:(r + 1) * 16], jnp.zeros((), bf16)) for r in range(RANK // 16)]
    return jnp.concatenate(parts, axis=0)


def stack_groups(poles_ref, stack_ref):
    for k in range(NB):
        stack_ref[k * RANK:(k + 1) * RANK, :] = poles_ref[:, k * TB:(k + 1) * TB]


def side_by_side(rows, i):
    return jnp.concatenate([rows[i:i + 1], rows[i + 1:i + 2]], axis=1)


def gather_rows(table_ref, stack_ref, place_ref, group_ref, hot_ref, store):
    def step(n, _):
        at = pl.multiple_of(n * FAR, FAR)
        places = place_ref[pl.ds(at, FAR), :]
        groups = group_ref[pl.ds(at, FAR), :]
        for i in range(0, FAR, 2):
            hot_ref[i // 2] = one_hot(table_ref, side_by_side(places, i))
            found = jnp.dot(stack_ref[...], hot_ref[i // 2], preferred_element_type=f32)
            found = pick_group(found, side_by_side(groups, i)).astype(bf16)
            store(at + i, found[:, :CAP])
            store(at + i + 1, found[:, CAP:])
        return 0

    lax.fori_loop(0, PEERS // FAR, step, 0)


GATHER_SCRATCH = [
    pltpu.VMEM((TB, LANES), bf16),
    pltpu.VMEM((STACK, TB), bf16),
    pltpu.VMEM((PEERS, CAP), f32),
    pltpu.VMEM((PEERS, CAP), f32),
    pltpu.VMEM((FAR // 2, TB, 2 * CAP), bf16),
]


def ops_kernel(far_op_ref, near_op_ref, m2l_ref, out_ref, wide_ref):
    count = m2l_ref.shape[1]
    slots = CAP + PAIRS
    names = jnp.concatenate([far_op_ref[...], near_op_ref[...]], axis=1)
    hot = (lax.broadcasted_iota(jnp.int32, (count, slots), 0) == names).astype(f32)
    hot = jnp.transpose(hot).astype(bf16)
    for r in range(0, RANK, 4):
        some = lax.dot_general(hot, m2l_ref[r * RANK:(r + 4) * RANK, :], NT, preferred_element_type=f32)
        for i in range(4):
            pair = some[:, (i // 2) * LANES:(i // 2 + 1) * LANES]
            if i % 2:
                pair = pltpu.roll(pair, RANK, 1)
            wide_ref[pl.ds(r + i, slots, stride=RANK), :] = pair

    def narrow(n, _):
        for i in range(8):
            s = n * 8 + i
            out_ref[s] = wide_ref[pl.ds(pl.multiple_of(s * RANK, RANK), RANK), :][:, :RANK].astype(bf16)
        return 0

    lax.fori_loop(0, slots // 8, narrow, 0)


def pick_ops(far_op, near_op, m2l):
    slots = CAP + PAIRS
    return pl.pallas_call(
        ops_kernel,
        out_shape=jax.ShapeDtypeStruct((slots, RANK, RANK), bf16),
        in_specs=[VMEM] * 3,
        out_specs=VMEM,
        scratch_shapes=[pltpu.VMEM((slots * RANK, LANES), f32)],
        compiler_params=pltpu.CompilerParams(vmem_limit_bytes=LIMIT),
        cost_estimate=pl.CostEstimate(flops=10**9, bytes_accessed=8 << 20, transcendentals=0),
        name="pick_ops",
    )(far_op.reshape(1, CAP), near_op.reshape(1, PAIRS), jnp.transpose(m2l, (1, 2, 0)).reshape(RANK * RANK, -1))


def up_kernel(child_ref, m2m_ref, source_ref, target_ref, poles_ref, send_ref,
              ask_place_ref, ask_group_ref, table_ref, stack_ref, place_ref, group_ref, hot_ref):
    fill_table(table_ref)
    ops = jnp.concatenate([m2m_ref[c] for c in range(CHILD)], axis=1)
    for s in range(0, BOX, 512):
        poles_ref[:, s:s + 512] = jnp.dot(
            ops, child_ref[:, s:s + 512], preferred_element_type=f32).astype(bf16)
    stack_groups(poles_ref, stack_ref)
    place_ref[...], group_ref[...] = split_index(source_ref[...])
    ask_place_ref[...], ask_group_ref[...] = split_index(target_ref[...])
    sub = lax.broadcasted_iota(jnp.int32, (16, CAP), 0)

    def store(q, block):
        send_ref[q, 0:RANK, :] = block
        ask = jnp.where(sub == 0, ask_place_ref[pl.ds(q, 1), :],
                        jnp.where(sub == 1, ask_group_ref[pl.ds(q, 1), :], 0.0))
        send_ref[q, RANK:SENT, :] = ask.astype(bf16)

    gather_rows(table_ref, stack_ref, place_ref, group_ref, hot_ref, store)


def upward(child, m2m, source, target):
    return pl.pallas_call(
        up_kernel,
        out_shape=(jax.ShapeDtypeStruct((RANK, BOX), bf16), jax.ShapeDtypeStruct((PEERS, SENT, CAP), bf16)),
        in_specs=[VMEM] * 4,
        out_specs=(VMEM, VMEM),
        scratch_shapes=[pltpu.VMEM((PEERS, CAP), f32), pltpu.VMEM((PEERS, CAP), f32)] + GATHER_SCRATCH,
        compiler_params=pltpu.CompilerParams(vmem_limit_bytes=LIMIT),
        cost_estimate=pl.CostEstimate(flops=10**10, bytes_accessed=6 << 20, transcendentals=0),
        name="upward",
    )(child, m2m, source, target)


def serve_kernel(poles_ref, received_ref, out_ref, table_ref, stack_ref, place_ref, group_ref, hot_ref):
    fill_table(table_ref)
    stack_groups(poles_ref, stack_ref)

    def unpack(n, _):
        for i in range(8):
            ask = received_ref[n * 8 + i, RANK:SENT, :].astype(f32)
            place_ref[pl.ds(n * 8 + i, 1), :] = ask[0:1]
            group_ref[pl.ds(n * 8 + i, 1), :] = ask[1:2]
        return 0

    lax.fori_loop(0, PEERS // 8, unpack, 0)

    def store(d, block):
        out_ref[d, :, :] = block

    gather_rows(table_ref, stack_ref, place_ref, group_ref, hot_ref, store)


def serve(poles, received):
    return pl.pallas_call(
        serve_kernel,
        out_shape=jax.ShapeDtypeStruct((PEERS, RANK, CAP), bf16),
        in_specs=[VMEM] * 2,
        out_specs=VMEM,
        scratch_shapes=GATHER_SCRATCH,
        compiler_params=pltpu.CompilerParams(vmem_limit_bytes=LIMIT),
        cost_estimate=pl.CostEstimate(flops=10**10, bytes_accessed=4 << 20, transcendentals=0),
        name="serve",
    )(poles, received)


def near_kernel(first, batches, poles_ref, partner_ref, ops_ref, out_ref,
                table_ref, stack_ref, place_ref, group_ref, hot_ref, spread_ref, sum_ref, both_ref):
    fill_table(table_ref)
    stack_groups(poles_ref, stack_ref)
    for b in range(NB):
        for j in range(BATCH):
            partner = partner_ref[first + j * batches:first + (j + 1) * batches, b * TB:(b + 1) * TB]
            lanes = slice((b * BATCH + j) * TB, (b * BATCH + j + 1) * TB)
            place_ref[:, lanes], group_ref[:, lanes] = split_index(partner)
    out_ref[...] = jnp.zeros(out_ref.shape, f32)

    def batch(n, _):
        ops = [ops_ref[CAP + first + j * batches + n] for j in range(BATCH)]
        ops = jnp.concatenate(ops + [jnp.transpose(op) for op in ops], axis=1)
        for b in range(NB):
            block = slice(b * TB, (b + 1) * TB)
            rows = (NB - b) * RANK
            for j in range(BATCH):
                lanes = slice((b * BATCH + j) * TB, (b * BATCH + j + 1) * TB)
                side = (b * BATCH + j) % SIDES
                place = place_ref[pl.ds(n, 1), lanes]
                group = group_ref[pl.ds(n, 1), lanes]
                hot_ref[side] = one_hot(table_ref, place)
                found = jnp.dot(stack_ref[b * RANK:, :], hot_ref[side], preferred_element_type=f32)
                both_ref[j * RANK:(j + 1) * RANK, block] = pick_group(found, group, b).astype(bf16)
                spread_ref[side, :rows, :] = spread_group(poles_ref[:, block], group, b)
                added = lax.dot_general(spread_ref[side, :rows, :], hot_ref[side], NT, preferred_element_type=f32)
                if b > 0:
                    added += sum_ref[j, b * RANK:, :]
                done = WIDE + j * RANK
                both_ref[done:done + RANK, block] = added[0:RANK].astype(bf16)
                if b < NB - 1:
                    sum_ref[j, (b + 1) * RANK:, :] = added[RANK:]
        out_ref[...] += jnp.dot(ops, both_ref[...], preferred_element_type=f32)
        return 0

    lax.fori_loop(0, batches, batch, 0)


def near(poles, partner, ops, first, batches):
    return pl.pallas_call(
        functools.partial(near_kernel, first, batches),
        out_shape=jax.ShapeDtypeStruct((RANK, BOX), f32),
        in_specs=[VMEM] * 3,
        out_specs=VMEM,
        scratch_shapes=[
            pltpu.VMEM((TB, LANES), bf16),
            pltpu.VMEM((STACK, TB), bf16),
            pltpu.VMEM((batches, BATCH * BOX), f32),
            pltpu.VMEM((batches, BATCH * BOX), f32),
            pltpu.VMEM((SIDES, TB, TB), bf16),
            pltpu.VMEM((SIDES, STACK, TB), bf16),
            pltpu.VMEM((BATCH, STACK, TB), f32),
            pltpu.VMEM((2 * WIDE, BOX), bf16),
        ],
        compiler_params=pltpu.CompilerParams(vmem_limit_bytes=LIMIT),
        cost_estimate=pl.CostEstimate(flops=10**9 * batches * BATCH, bytes_accessed=6 << 20, transcendentals=0),
        name="near",
    )(poles, partner, ops)


def down_kernel(near_a_ref, near_b_ref, served_ref, own_ref, source_ref, ops_ref, m2m_ref, out_ref,
                table_ref, place_ref, group_ref, hot_ref, spread_ref, total_ref, local_ref):
    fill_table(table_ref)
    place, group = split_index(source_ref[...])
    place_ref[...] = jnp.transpose(place)
    group_ref[...] = jnp.transpose(group)
    total_ref[...] = jnp.zeros(total_ref.shape, f32)

    def step(n, _):
        at = pl.multiple_of(n * FAR, FAR)
        source_places = place_ref[pl.ds(at, FAR), :]
        source_groups = group_ref[pl.ds(at, FAR), :]
        for i in range(0, FAR, 2):
            back, ahead, places, groups = [], [], [], []
            for k in range(2):
                c = at + i + k
                op = ops_ref[c]
                ahead.append(jnp.dot(op, served_ref[c], preferred_element_type=f32).astype(bf16))
                back.append(lax.dot_general(op, own_ref[c, 0:RANK, :], TN, preferred_element_type=f32).astype(bf16))
                ask = own_ref[c, RANK:SENT, :].astype(f32)
                places.append(ask[0:1])
                groups.append(ask[1:2])
            lanes = slice(2 * i * PEERS, (2 * i + 2) * PEERS)
            hot_ref[:, lanes] = one_hot(table_ref, side_by_side(source_places, i))
            spread_ref[:, lanes] = spread_group(jnp.concatenate(ahead, axis=1), side_by_side(source_groups, i))
            lanes = slice((2 * i + 2) * PEERS, (2 * i + 4) * PEERS)
            hot_ref[:, lanes] = one_hot(table_ref, jnp.concatenate(places, axis=1))
            spread_ref[:, lanes] = spread_group(jnp.concatenate(back, axis=1), jnp.concatenate(groups, axis=1))
        total_ref[...] += lax.dot_general(spread_ref[...], hot_ref[...], NT, preferred_element_type=f32)
        return 0

    lax.fori_loop(0, CAP // FAR, step, 0)
    ops = jnp.concatenate([m2m_ref[c] for c in range(CHILD)], axis=1)
    for k in range(NB):
        cols = slice(k * TB, (k + 1) * TB)
        far = total_ref[k * RANK:(k + 1) * RANK, :]
        local_ref[:, cols] = (near_a_ref[:, cols] + near_b_ref[:, cols] + far).astype(bf16)
        out_ref[:, cols] = lax.dot_general(
            ops, local_ref[:, cols], TN, preferred_element_type=f32).astype(bf16)


def downward(near_a, near_b, served, own, source, ops, m2m):
    return pl.pallas_call(
        down_kernel,
        out_shape=jax.ShapeDtypeStruct((CHILD * RANK, BOX), bf16),
        in_specs=[VMEM] * 7,
        out_specs=VMEM,
        scratch_shapes=[
            pltpu.VMEM((TB, LANES), bf16),
            pltpu.VMEM((CAP, PEERS), f32),
            pltpu.VMEM((CAP, PEERS), f32),
            pltpu.VMEM((TB, 2 * FAR * PEERS), bf16),
            pltpu.VMEM((STACK, 2 * FAR * PEERS), bf16),
            pltpu.VMEM((STACK, TB), f32),
            pltpu.VMEM((RANK, BOX), bf16),
        ],
        compiler_params=pltpu.CompilerParams(vmem_limit_bytes=LIMIT),
        cost_estimate=pl.CostEstimate(flops=2 * 10**10, bytes_accessed=16 << 20, transcendentals=0),
        name="downward",
    )(near_a, near_b, served, own, source, ops, m2m)


def on_device(child_poles, m2m_ops, m2l_ops, near_partner, near_op, far_source, far_target, far_op):
    child = child_poles.reshape(CHILD * RANK, BOX)
    source = far_source[0]
    poles, send = upward(child, m2m_ops, source, far_target[0])
    received = lax.all_to_all(send, ("curve", "sub"), split_axis=0, concat_axis=0, tiled=True)
    ops = pick_ops(far_op, near_op, m2l_ops)
    half = PAIRS // BATCH // 2
    near_a = near(poles, near_partner, ops, 0, half)
    answer = serve(poles, received)
    fetched = lax.all_to_all(answer, ("curve", "sub"), split_axis=0, concat_axis=0, tiled=True)
    near_b = near(poles, near_partner, ops, half * BATCH, PAIRS // BATCH - half)
    own = jnp.transpose(received, (2, 1, 0))
    served = jnp.transpose(fetched, (2, 1, 0))
    out = downward(near_a, near_b, served, own, source, ops, m2m_ops)
    return out.reshape(CHILD, RANK, BOX)


def solution(mesh):
    placed = (
        P(None, None, ("curve", "sub")),
        P(),
        P(),
        P(None, ("curve", "sub")),
        P(),
        P(("curve", "sub"), None, None),
        P(("curve", "sub"), None, None),
        P(),
    )
    return jax.shard_map(
        on_device,
        mesh=mesh,
        in_specs=placed,
        out_specs=P(None, None, ("curve", "sub")),
        check_vma=False,
    )
```

```python
import functools

import jax
import jax.numpy as jnp
from jax import lax
from jax.experimental import pallas as pl
from jax.experimental.pallas import tpu as pltpu
from jax.sharding import PartitionSpec as P

RANK = 64
CHILD = 8
BOX = 2048
PEERS = 128
CAP = 128
PAIRS = 88
LANES = 128
TB = 256
NB = BOX // TB
STACK = NB * RANK
BATCH = 8
WIDE = BATCH * RANK
SIDES = 4
BY_LANE = 3
FAR = 8
EMPTY = 512
SENT = RANK + 16
f32 = jnp.float32
bf16 = jnp.bfloat16
VMEM = pl.BlockSpec(memory_space=pltpu.VMEM)
LIMIT = 56 * 2**20
ANY = pl.BlockSpec(memory_space=pl.ANY)
NT = (((1,), (1,)), ((), ()))
TN = (((0,), (0,)), ((), ()))


def fill_table(table_ref):
    table_ref[...] = lax.broadcasted_iota(jnp.int32, table_ref.shape, 0).astype(f32).astype(bf16)


def split_index(index):
    group = index >> 8
    place = jnp.where(index >= 0, index - group * TB, EMPTY)
    return place.astype(f32), jnp.maximum(group, 0).astype(f32)


def one_hot(table_ref, place):
    n = place.shape[1]
    row = jnp.broadcast_to(place, (16, n)).astype(bf16)
    parts = []
    for r in range(TB // 16):
        here = table_ref[r * 16:(r + 1) * 16, :]
        here = jnp.concatenate([here] * (n // LANES), axis=1)
        parts.append(jnp.where(here == row, jnp.ones((), bf16), jnp.zeros((), bf16)))
    return jnp.concatenate(parts, axis=0)


def pick_group(stacked, group, low=0):
    out = stacked[0:RANK]
    for k in range(low + 1, NB):
        out = jnp.where(group == float(k), stacked[(k - low) * RANK:(k - low + 1) * RANK], out)
    return out


def spread_group(values, group, low=0):
    n = values.shape[1]
    row = jnp.broadcast_to(group, (16, n)).astype(bf16)
    parts = []
    for k in range(low, NB):
        mask = row == jnp.array(k, bf16)
        parts += [jnp.where(mask, values[r * 16:(r + 1) * 16], jnp.zeros((), bf16)) for r in range(RANK // 16)]
    return jnp.concatenate(parts, axis=0)


def stack_groups(poles_ref, stack_ref):
    for k in range(NB):
        stack_ref[k * RANK:(k + 1) * RANK, :] = poles_ref[:, k * TB:(k + 1) * TB]


def side_by_side(rows, i):
    return jnp.concatenate([rows[i:i + 1], rows[i + 1:i + 2]], axis=1)


def gather_rows(table_ref, stack_ref, place_ref, group_ref, hot_ref, store, flush):
    def step(n, _):
        at = pl.multiple_of(n * FAR, FAR)
        places = place_ref[pl.ds(at, FAR), :]
        groups = group_ref[pl.ds(at, FAR), :]
        for i in range(0, FAR, 2):
            hot_ref[i // 2] = one_hot(table_ref, side_by_side(places, i))
            found = jnp.dot(stack_ref[...], hot_ref[i // 2], preferred_element_type=f32)
            found = pick_group(found, side_by_side(groups, i)).astype(bf16)
            store(at + i, found[:, :CAP])
            store(at + i + 1, found[:, CAP:])
        flush(at)
        return 0

    lax.fori_loop(0, PEERS // FAR, step, 0)


GATHER_SCRATCH = [
    pltpu.VMEM((TB, LANES), bf16),
    pltpu.VMEM((STACK, TB), bf16),
    pltpu.VMEM((PEERS, CAP), f32),
    pltpu.VMEM((PEERS, CAP), f32),
    pltpu.VMEM((FAR // 2, TB, 2 * CAP), bf16),
]


def select_ops(far_op_ref, near_op_ref, m2l_ref, ready, far_ref, near_ref, wide_ref):
    count = m2l_ref.shape[1]
    slots = CAP + PAIRS
    names = jnp.concatenate([far_op_ref[...], near_op_ref[...]], axis=1)
    hot = (lax.broadcasted_iota(jnp.int32, (count, slots), 0) == names).astype(f32)
    hot = jnp.transpose(hot).astype(bf16)
    ready()
    for r in range(0, RANK, 4):
        some = lax.dot_general(hot, m2l_ref[r * RANK:(r + 4) * RANK, :], NT, preferred_element_type=f32)
        for i in range(4):
            pair = some[:, (i // 2) * LANES:(i // 2 + 1) * LANES]
            if i % 2:
                pair = pltpu.roll(pair, RANK, 1)
            wide_ref[pl.ds(r + i, slots, stride=RANK), :] = pair
    for out_ref, start in ((near_ref, CAP), (far_ref, 0)):
        def narrow(n, _):
            for i in range(8):
                s = n * 8 + i
                row = pl.multiple_of((start + s) * RANK, RANK)
                out_ref[s] = wide_ref[pl.ds(row, RANK), :][:, :RANK].astype(bf16)
            return 0

        lax.fori_loop(0, out_ref.shape[0] // 8, narrow, 0)


def up_kernel(child_any, source_any, target_any, m2l_any, m2m_ref, far_op_ref, near_op_ref,
              poles_any, send_any, far_any, near_any,
              child_ref, source_ref, target_ref, m2l_ref, poles_ref, send_ref, far_ref, near_ref, wide_ref,
              in_sem, out_sem, ask_place_ref, ask_group_ref, table_ref, stack_ref, place_ref, group_ref, hot_ref):
    part = BOX // 4
    copies = [pltpu.make_async_copy(child_any.at[:, i * part:(i + 1) * part],
                                    child_ref.at[:, i * part:(i + 1) * part], in_sem.at[i]) for i in range(4)]
    copies += [pltpu.make_async_copy(source_any, source_ref, in_sem.at[4]),
               pltpu.make_async_copy(target_any, target_ref, in_sem.at[5]),
               pltpu.make_async_copy(m2l_any, m2l_ref, in_sem.at[6])]
    for copy in copies:
        copy.start()
    fill_table(table_ref)
    ops = jnp.concatenate([m2m_ref[c] for c in range(CHILD)], axis=1)
    for i in range(4):
        cols = slice(i * part, (i + 1) * part)
        copies[i].wait()
        poles_ref[:, cols] = jnp.dot(ops, child_ref[:, cols], preferred_element_type=f32).astype(bf16)
    poles_out = pltpu.make_async_copy(poles_ref, poles_any, out_sem.at[0])
    poles_out.start()
    stack_groups(poles_ref, stack_ref)
    copies[4].wait()
    copies[5].wait()
    place_ref[...], group_ref[...] = split_index(source_ref[...])
    ask_place_ref[...], ask_group_ref[...] = split_index(target_ref[...])
    sub = lax.broadcasted_iota(jnp.int32, (16, CAP), 0)

    def store(q, block):
        send_ref[q, 0:RANK, :] = block
        ask = jnp.where(sub == 0, ask_place_ref[pl.ds(q, 1), :],
                        jnp.where(sub == 1, ask_group_ref[pl.ds(q, 1), :], 0.0))
        send_ref[q, RANK:SENT, :] = ask.astype(bf16)

    def flush(q):
        pltpu.make_async_copy(send_ref.at[pl.ds(q, FAR)], send_any.at[pl.ds(q, FAR)], out_sem.at[1]).start()

    gather_rows(table_ref, stack_ref, place_ref, group_ref, hot_ref, store, flush)
    select_ops(far_op_ref, near_op_ref, m2l_ref, copies[6].wait, far_ref, near_ref, wide_ref)
    near_out = pltpu.make_async_copy(near_ref, near_any, out_sem.at[2])
    far_out = pltpu.make_async_copy(far_ref, far_any, out_sem.at[3])
    near_out.start()
    far_out.start()
    poles_out.wait()
    pltpu.make_async_copy(send_ref, send_any, out_sem.at[1]).wait()
    near_out.wait()
    far_out.wait()


def upward(child, m2m, source, target, far_op, near_op, m2l):
    slots = CAP + PAIRS
    flat = jnp.transpose(m2l, (1, 2, 0)).reshape(RANK * RANK, -1)
    out_shape = (
        jax.ShapeDtypeStruct((RANK, BOX), bf16),
        jax.ShapeDtypeStruct((PEERS, SENT, CAP), bf16),
        jax.ShapeDtypeStruct((CAP, RANK, RANK), bf16),
        jax.ShapeDtypeStruct((PAIRS, RANK, RANK), bf16),
    )
    return pl.pallas_call(
        up_kernel,
        out_shape=out_shape,
        in_specs=[ANY] * 4 + [VMEM] * 3,
        out_specs=(ANY,) * 4,
        scratch_shapes=[
            pltpu.VMEM(child.shape, bf16),
            pltpu.VMEM(source.shape, jnp.int32),
            pltpu.VMEM(target.shape, jnp.int32),
            pltpu.VMEM(flat.shape, bf16),
        ] + [pltpu.VMEM(o.shape, o.dtype) for o in out_shape] + [
            pltpu.VMEM((slots * RANK, LANES), f32),
            pltpu.SemaphoreType.DMA((7,)),
            pltpu.SemaphoreType.DMA((4,)),
            pltpu.VMEM((PEERS, CAP), f32),
            pltpu.VMEM((PEERS, CAP), f32),
        ] + GATHER_SCRATCH,
        compiler_params=pltpu.CompilerParams(vmem_limit_bytes=LIMIT),
        cost_estimate=pl.CostEstimate(flops=10**10, bytes_accessed=12 << 20, transcendentals=0),
        name="upward",
    )(child, source, target, flat, m2m, far_op.reshape(1, CAP), near_op.reshape(1, PAIRS))


def serve_kernel(poles_ref, received_any, out_any, out_ref, ask_ref, in_sem, out_sem,
                 table_ref, stack_ref, place_ref, group_ref, hot_ref):
    asked = pltpu.make_async_copy(received_any.at[:, RANK:SENT, :], ask_ref, in_sem)
    asked.start()
    fill_table(table_ref)
    stack_groups(poles_ref, stack_ref)
    asked.wait()

    def unpack(n, _):
        for i in range(8):
            ask = ask_ref[n * 8 + i].astype(f32)
            place_ref[pl.ds(n * 8 + i, 1), :] = ask[0:1]
            group_ref[pl.ds(n * 8 + i, 1), :] = ask[1:2]
        return 0

    lax.fori_loop(0, PEERS // 8, unpack, 0)

    def store(d, block):
        out_ref[d, :, :] = block

    def flush(d):
        pltpu.make_async_copy(out_ref.at[pl.ds(d, FAR)], out_any.at[pl.ds(d, FAR)], out_sem).start()

    gather_rows(table_ref, stack_ref, place_ref, group_ref, hot_ref, store, flush)
    pltpu.make_async_copy(out_ref, out_any, out_sem).wait()


def serve(poles, received):
    return pl.pallas_call(
        serve_kernel,
        out_shape=jax.ShapeDtypeStruct((PEERS, RANK, CAP), bf16),
        in_specs=[VMEM, ANY],
        out_specs=ANY,
        scratch_shapes=[
            pltpu.VMEM((PEERS, RANK, CAP), bf16),
            pltpu.VMEM((PEERS, SENT - RANK, CAP), bf16),
            pltpu.SemaphoreType.DMA,
            pltpu.SemaphoreType.DMA,
        ] + GATHER_SCRATCH,
        compiler_params=pltpu.CompilerParams(vmem_limit_bytes=LIMIT),
        cost_estimate=pl.CostEstimate(flops=10**10, bytes_accessed=4 << 20, transcendentals=0),
        name="serve",
    )(poles, received)


def pick_lanes(poles_ref, lane, chunk, b):
    columns = []
    for t in range(TB // LANES):
        first = b * (TB // LANES) + t
        at = jnp.broadcast_to(lane[:, t * LANES:(t + 1) * LANES], (8, LANES)).astype(jnp.int32)
        where = jnp.broadcast_to(chunk[:, t * LANES:(t + 1) * LANES], (8, LANES))
        found = [jnp.zeros((8, LANES), f32)] * (RANK // 8)
        for k in range(first, BOX // LANES):
            mask = where == float(k)
            for r in range(RANK // 8):
                moved = jnp.take_along_axis(poles_ref[r * 8:(r + 1) * 8, k * LANES:(k + 1) * LANES], at, axis=1)
                found[r] = jnp.where(mask, moved, found[r])
        columns.append(jnp.concatenate(found, axis=0))
    return jnp.concatenate(columns, axis=1)


def near_kernel(first, batches, poles_ref, partner_ref, ops_ref, out_ref,
                table_ref, stack_ref, place_ref, group_ref, lane_ref, chunk_ref, poles32_ref, hot_ref, spread_ref,
                sum_ref, both_ref):
    fill_table(table_ref)
    poles32_ref[...] = poles_ref[...].astype(f32)
    stack_groups(poles_ref, stack_ref)
    for b in range(NB):
        for j in range(BATCH):
            partner = partner_ref[first + j * batches:first + (j + 1) * batches, b * TB:(b + 1) * TB]
            lanes = slice((b * BATCH + j) * TB, (b * BATCH + j + 1) * TB)
            place_ref[:, lanes], group_ref[:, lanes] = split_index(partner)
            if b >= BY_LANE:
                lane_ref[:, lanes] = (partner & (LANES - 1)).astype(f32)
                chunk_ref[:, lanes] = (partner >> 7).astype(f32)
    out_ref[...] = jnp.zeros(out_ref.shape, f32)

    def batch(n, _):
        ops = [ops_ref[first + j * batches + n] for j in range(BATCH)]
        ops = jnp.concatenate(ops + [jnp.transpose(op) for op in ops], axis=1)
        for b in range(NB):
            block = slice(b * TB, (b + 1) * TB)
            rows = (NB - b) * RANK
            for j in range(BATCH):
                lanes = slice((b * BATCH + j) * TB, (b * BATCH + j + 1) * TB)
                side = (b * BATCH + j) % SIDES
                place = place_ref[pl.ds(n, 1), lanes]
                group = group_ref[pl.ds(n, 1), lanes]
                hot_ref[side] = one_hot(table_ref, place)
                if b < BY_LANE:
                    found = jnp.dot(stack_ref[b * RANK:, :], hot_ref[side], preferred_element_type=f32)
                    both_ref[j * RANK:(j + 1) * RANK, block] = pick_group(found, group, b).astype(bf16)
                o = NB - 1 - b
                if o >= BY_LANE:
                    lanes = slice((o * BATCH + j) * TB, (o * BATCH + j + 1) * TB)
                    picked = pick_lanes(poles32_ref, lane_ref[pl.ds(n, 1), lanes], chunk_ref[pl.ds(n, 1), lanes], o)
                    both_ref[j * RANK:(j + 1) * RANK, o * TB:(o + 1) * TB] = picked.astype(bf16)
                spread_ref[side, :rows, :] = spread_group(poles_ref[:, block], group, b)
                added = lax.dot_general(spread_ref[side, :rows, :], hot_ref[side], NT, preferred_element_type=f32)
                if b > 0:
                    added += sum_ref[j, b * RANK:, :]
                done = WIDE + j * RANK
                both_ref[done:done + RANK, block] = added[0:RANK].astype(bf16)
                if b < NB - 1:
                    sum_ref[j, (b + 1) * RANK:, :] = added[RANK:]
        out_ref[...] += jnp.dot(ops, both_ref[...], preferred_element_type=f32)
        return 0

    lax.fori_loop(0, batches, batch, 0)


def near(poles, partner, ops, first, batches):
    return pl.pallas_call(
        functools.partial(near_kernel, first, batches),
        out_shape=jax.ShapeDtypeStruct((RANK, BOX), f32),
        in_specs=[VMEM] * 3,
        out_specs=VMEM,
        scratch_shapes=[
            pltpu.VMEM((TB, LANES), bf16),
            pltpu.VMEM((STACK, TB), bf16),
            pltpu.VMEM((batches, BATCH * BOX), f32),
            pltpu.VMEM((batches, BATCH * BOX), f32),
            pltpu.VMEM((batches, BATCH * BOX), f32),
            pltpu.VMEM((batches, BATCH * BOX), f32),
            pltpu.VMEM((RANK, BOX), f32),
            pltpu.VMEM((SIDES, TB, TB), bf16),
            pltpu.VMEM((SIDES, STACK, TB), bf16),
            pltpu.VMEM((BATCH, STACK, TB), f32),
            pltpu.VMEM((2 * WIDE, BOX), bf16),
        ],
        compiler_params=pltpu.CompilerParams(vmem_limit_bytes=LIMIT),
        cost_estimate=pl.CostEstimate(flops=10**9 * batches * BATCH, bytes_accessed=6 << 20, transcendentals=0),
        name="near",
    )(poles, partner, ops)


def down_kernel(served_any, own_any, near_a_ref, near_b_ref, source_ref, ops_ref, m2m_ref, out_any,
                served_ref, own_ref, out_ref, in_sem, out_sem,
                table_ref, place_ref, group_ref, hot_ref, spread_ref, total_ref, local_ref):
    def fetch(n):
        rows = pl.ds(n * FAR, FAR)
        return (pltpu.make_async_copy(served_any.at[rows], served_ref.at[rows], in_sem.at[0, n]),
                pltpu.make_async_copy(own_any.at[rows], own_ref.at[rows], in_sem.at[1, n]))

    for n in range(CAP // FAR):
        for copy in fetch(n):
            copy.start()
    fill_table(table_ref)
    place, group = split_index(source_ref[...])
    place_ref[...] = jnp.transpose(place)
    group_ref[...] = jnp.transpose(group)
    total_ref[...] = jnp.zeros(total_ref.shape, f32)

    def step(n, _):
        at = pl.multiple_of(n * FAR, FAR)
        for copy in fetch(n):
            copy.wait()
        source_places = place_ref[pl.ds(at, FAR), :]
        source_groups = group_ref[pl.ds(at, FAR), :]

        for i in range(0, FAR, 2):
            back, ahead, places, groups = [], [], [], []
            for k in range(2):
                c = at + i + k
                op = ops_ref[c]
                ahead.append(jnp.dot(op, served_ref[c], preferred_element_type=f32).astype(bf16))
                back.append(lax.dot_general(op, own_ref[c, 0:RANK, :], TN, preferred_element_type=f32).astype(bf16))
                ask = own_ref[c, RANK:SENT, :].astype(f32)
                places.append(ask[0:1])
                groups.append(ask[1:2])
            lanes = slice(2 * i * PEERS, (2 * i + 2) * PEERS)
            hot_ref[:, lanes] = one_hot(table_ref, side_by_side(source_places, i))
            spread_ref[:, lanes] = spread_group(jnp.concatenate(ahead, axis=1), side_by_side(source_groups, i))
            lanes = slice((2 * i + 2) * PEERS, (2 * i + 4) * PEERS)
            hot_ref[:, lanes] = one_hot(table_ref, jnp.concatenate(places, axis=1))
            spread_ref[:, lanes] = spread_group(jnp.concatenate(back, axis=1), jnp.concatenate(groups, axis=1))
        total_ref[...] += lax.dot_general(spread_ref[...], hot_ref[...], NT, preferred_element_type=f32)
        return 0

    lax.fori_loop(0, CAP // FAR, step, 0)
    ops = jnp.concatenate([m2m_ref[c] for c in range(CHILD)], axis=1)
    for k in range(NB):
        cols = slice(k * TB, (k + 1) * TB)
        far = total_ref[k * RANK:(k + 1) * RANK, :]
        local_ref[:, cols] = (near_a_ref[:, cols] + near_b_ref[:, cols] + far).astype(bf16)
        out_ref[:, cols] = lax.dot_general(
            ops, local_ref[:, cols], TN, preferred_element_type=f32).astype(bf16)
        if k % 4 == 3:
            cols = slice((k - 3) * TB, (k + 1) * TB)
            pltpu.make_async_copy(out_ref.at[:, cols], out_any.at[:, cols], out_sem).start()
    pltpu.make_async_copy(out_ref, out_any, out_sem).wait()


def downward(near_a, near_b, served, own, source, ops, m2m):
    return pl.pallas_call(
        down_kernel,
        out_shape=jax.ShapeDtypeStruct((CHILD * RANK, BOX), bf16),
        in_specs=[ANY] * 2 + [VMEM] * 5,
        out_specs=ANY,
        scratch_shapes=[
            pltpu.VMEM(served.shape, bf16),
            pltpu.VMEM(own.shape, bf16),
            pltpu.VMEM((CHILD * RANK, BOX), bf16),
            pltpu.SemaphoreType.DMA((2, CAP // FAR)),
            pltpu.SemaphoreType.DMA,
            pltpu.VMEM((TB, LANES), bf16),
            pltpu.VMEM((CAP, PEERS), f32),
            pltpu.VMEM((CAP, PEERS), f32),
            pltpu.VMEM((TB, 2 * FAR * PEERS), bf16),
            pltpu.VMEM((STACK, 2 * FAR * PEERS), bf16),
            pltpu.VMEM((STACK, TB), f32),
            pltpu.VMEM((RANK, BOX), bf16),
        ],
        compiler_params=pltpu.CompilerParams(vmem_limit_bytes=LIMIT),
        cost_estimate=pl.CostEstimate(flops=2 * 10**10, bytes_accessed=16 << 20, transcendentals=0),
        name="downward",
    )(served, own, near_a, near_b, source, ops, m2m)


def on_device(child_poles, m2m_ops, m2l_ops, near_partner, near_op, far_source, far_target, far_op):
    child = child_poles.reshape(CHILD * RANK, BOX)
    source = far_source[0]
    poles, send, far_ops, near_ops = upward(child, m2m_ops, source, far_target[0], far_op, near_op, m2l_ops)
    received = lax.all_to_all(send, ("curve", "sub"), split_axis=0, concat_axis=0, tiled=True)
    half = (PAIRS // BATCH + 1) // 2
    near_a = near(poles, near_partner, near_ops, 0, half)
    answer = serve(poles, received)
    fetched = lax.all_to_all(answer, ("curve", "sub"), split_axis=0, concat_axis=0, tiled=True)
    near_b = near(poles, near_partner, near_ops, half * BATCH, PAIRS // BATCH - half)
    own = jnp.transpose(received, (2, 1, 0))
    served = jnp.transpose(fetched, (2, 1, 0))
    out = downward(near_a, near_b, served, own, source, far_ops, m2m_ops)
    return out.reshape(CHILD, RANK, BOX)


def solution(mesh):
    placed = (
        P(None, None, ("curve", "sub")),
        P(),
        P(),
        P(None, ("curve", "sub")),
        P(),
        P(("curve", "sub"), None, None),
        P(("curve", "sub"), None, None),
        P(),
    )
    return jax.shard_map(
        on_device,
        mesh=mesh,
        in_specs=placed,
        out_specs=P(None, None, ("curve", "sub")),
        check_vma=False,
    )
```

```python
import functools

import jax
import jax.numpy as jnp
from jax import lax
from jax.experimental import pallas as pl
from jax.experimental.pallas import tpu as pltpu
from jax.sharding import PartitionSpec as P

RANK = 64
CHILD = 8
BOX = 2048
PEERS = 128
CAP = 128
PAIRS = 88
LANES = 128
TB = 256
NB = BOX // TB
STACK = NB * RANK
BATCH = 8
WIDE = BATCH * RANK
SIDES = 4
BY_LANE = 3
FAR = 8
EMPTY = 512
SENT = RANK + 16
f32 = jnp.float32
bf16 = jnp.bfloat16
VMEM = pl.BlockSpec(memory_space=pltpu.VMEM)
LIMIT = 56 * 2**20
ANY = pl.BlockSpec(memory_space=pl.ANY)
NT = (((1,), (1,)), ((), ()))
TN = (((0,), (0,)), ((), ()))


def fill_table(table_ref):
    table_ref[...] = lax.broadcasted_iota(jnp.int32, table_ref.shape, 0).astype(f32).astype(bf16)


def split_index(index):
    group = index >> 8
    place = jnp.where(index >= 0, index - group * TB, EMPTY)
    return place.astype(f32), jnp.maximum(group, 0).astype(f32)


def one_hot(table_ref, place):
    n = place.shape[1]
    row = jnp.broadcast_to(place, (16, n)).astype(bf16)
    parts = []
    for r in range(TB // 16):
        here = table_ref[r * 16:(r + 1) * 16, :]
        here = jnp.concatenate([here] * (n // LANES), axis=1)
        parts.append(jnp.where(here == row, jnp.ones((), bf16), jnp.zeros((), bf16)))
    return jnp.concatenate(parts, axis=0)


def pick_group(stacked, group, low=0):
    out = stacked[0:RANK]
    for k in range(low + 1, NB):
        out = jnp.where(group == float(k), stacked[(k - low) * RANK:(k - low + 1) * RANK], out)
    return out


def spread_group(values, group, low=0):
    n = values.shape[1]
    row = jnp.broadcast_to(group, (16, n)).astype(bf16)
    parts = []
    for k in range(low, NB):
        mask = row == jnp.array(k, bf16)
        parts += [jnp.where(mask, values[r * 16:(r + 1) * 16], jnp.zeros((), bf16)) for r in range(RANK // 16)]
    return jnp.concatenate(parts, axis=0)


def stack_groups(poles_ref, stack_ref):
    for k in range(NB):
        stack_ref[k * RANK:(k + 1) * RANK, :] = poles_ref[:, k * TB:(k + 1) * TB]


def side_by_side(rows, i):
    return jnp.concatenate([rows[i:i + 1], rows[i + 1:i + 2]], axis=1)


def gather_rows(table_ref, stack_ref, place_ref, group_ref, hot_ref, store, flush):
    def step(n, _):
        at = pl.multiple_of(n * FAR, FAR)
        places = place_ref[pl.ds(at, FAR), :]
        groups = group_ref[pl.ds(at, FAR), :]
        for i in range(0, FAR, 2):
            hot_ref[i // 2] = one_hot(table_ref, side_by_side(places, i))
            found = jnp.dot(stack_ref[...], hot_ref[i // 2], preferred_element_type=f32)
            found = pick_group(found, side_by_side(groups, i)).astype(bf16)
            store(at + i, found[:, :CAP])
            store(at + i + 1, found[:, CAP:])
        flush(at)
        return 0

    lax.fori_loop(0, PEERS // FAR, step, 0)


GATHER_SCRATCH = [
    pltpu.VMEM((TB, LANES), bf16),
    pltpu.VMEM((STACK, TB), bf16),
    pltpu.VMEM((PEERS, CAP), f32),
    pltpu.VMEM((PEERS, CAP), f32),
    pltpu.VMEM((FAR // 2, TB, 2 * CAP), bf16),
]


def select_ops(far_op_ref, near_op_ref, m2l_ref, ready, far_ref, near_ref):
    count = m2l_ref.shape[1]
    names = jnp.concatenate([far_op_ref[...], near_op_ref[...]], axis=1)
    hot = (lax.broadcasted_iota(jnp.int32, (count, CAP + PAIRS), 0) == names).astype(f32)
    hot = jnp.transpose(hot).astype(bf16)
    ready()
    for m in range(0, RANK // 2, 2):
        rows = [m2l_ref[r * RANK:(r + 1) * RANK, :] for r in (m, m + RANK // 2, m + 1, m + 1 + RANK // 2)]
        some = lax.dot_general(hot, jnp.concatenate(rows, axis=0), NT, preferred_element_type=f32)
        for i in range(2):
            pair = some[:, i * LANES:(i + 1) * LANES]
            far_ref[(m + i) * CAP:(m + i + 1) * CAP, :] = pair[:CAP]
            near_ref[(m + i) * PAIRS:(m + i + 1) * PAIRS, :] = pair[CAP:]


def take_op(ops_ref, s, slots):
    pairs = ops_ref[pl.ds(s, RANK // 2, stride=slots), :]
    return jnp.concatenate([pairs[:, :RANK], pairs[:, RANK:]], axis=0).astype(bf16)


def up_kernel(child_any, source_any, target_any, m2l_any, m2m_ref, far_op_ref, near_op_ref,
              poles_any, send_any, far_any, near_any,
              child_ref, source_ref, target_ref, m2l_ref, poles_ref, send_ref, far_ref, near_ref,
              in_sem, out_sem, ask_place_ref, ask_group_ref, table_ref, stack_ref, place_ref, group_ref, hot_ref):
    part = BOX // 4
    copies = [pltpu.make_async_copy(child_any.at[:, i * part:(i + 1) * part],
                                    child_ref.at[:, i * part:(i + 1) * part], in_sem.at[i]) for i in range(4)]
    copies += [pltpu.make_async_copy(source_any, source_ref, in_sem.at[4]),
               pltpu.make_async_copy(target_any, target_ref, in_sem.at[5]),
               pltpu.make_async_copy(m2l_any, m2l_ref, in_sem.at[6])]
    for copy in copies:
        copy.start()
    fill_table(table_ref)
    ops = jnp.concatenate([m2m_ref[c] for c in range(CHILD)], axis=1)
    for i in range(4):
        cols = slice(i * part, (i + 1) * part)
        copies[i].wait()
        poles_ref[:, cols] = jnp.dot(ops, child_ref[:, cols], preferred_element_type=f32).astype(bf16)
    poles_out = pltpu.make_async_copy(poles_ref, poles_any, out_sem.at[0])
    poles_out.start()
    stack_groups(poles_ref, stack_ref)
    copies[4].wait()
    copies[5].wait()
    place_ref[...], group_ref[...] = split_index(source_ref[...])
    ask_place_ref[...], ask_group_ref[...] = split_index(target_ref[...])
    sub = lax.broadcasted_iota(jnp.int32, (16, CAP), 0)

    def store(q, block):
        send_ref[q, 0:RANK, :] = block
        ask = jnp.where(sub == 0, ask_place_ref[pl.ds(q, 1), :],
                        jnp.where(sub == 1, ask_group_ref[pl.ds(q, 1), :], 0.0))
        send_ref[q, RANK:SENT, :] = ask.astype(bf16)

    def flush(q):
        pltpu.make_async_copy(send_ref.at[pl.ds(q, FAR)], send_any.at[pl.ds(q, FAR)], out_sem.at[1]).start()

    gather_rows(table_ref, stack_ref, place_ref, group_ref, hot_ref, store, flush)
    select_ops(far_op_ref, near_op_ref, m2l_ref, copies[6].wait, far_ref, near_ref)
    near_out = pltpu.make_async_copy(near_ref, near_any, out_sem.at[2])
    far_out = pltpu.make_async_copy(far_ref, far_any, out_sem.at[3])
    near_out.start()
    far_out.start()
    poles_out.wait()
    pltpu.make_async_copy(send_ref, send_any, out_sem.at[1]).wait()
    near_out.wait()
    far_out.wait()


def upward(child, m2m, source, target, far_op, near_op, m2l):
    flat = jnp.transpose(m2l, (1, 2, 0)).reshape(RANK * RANK, -1)
    out_shape = (
        jax.ShapeDtypeStruct((RANK, BOX), bf16),
        jax.ShapeDtypeStruct((PEERS, SENT, CAP), bf16),
        jax.ShapeDtypeStruct((RANK // 2 * CAP, LANES), f32),
        jax.ShapeDtypeStruct((RANK // 2 * PAIRS, LANES), f32),
    )
    return pl.pallas_call(
        up_kernel,
        out_shape=out_shape,
        in_specs=[ANY] * 4 + [VMEM] * 3,
        out_specs=(ANY,) * 4,
        scratch_shapes=[
            pltpu.VMEM(child.shape, bf16),
            pltpu.VMEM(source.shape, jnp.int32),
            pltpu.VMEM(target.shape, jnp.int32),
            pltpu.VMEM(flat.shape, bf16),
        ] + [pltpu.VMEM(o.shape, o.dtype) for o in out_shape] + [
            pltpu.SemaphoreType.DMA((7,)),
            pltpu.SemaphoreType.DMA((4,)),
            pltpu.VMEM((PEERS, CAP), f32),
            pltpu.VMEM((PEERS, CAP), f32),
        ] + GATHER_SCRATCH,
        compiler_params=pltpu.CompilerParams(vmem_limit_bytes=LIMIT),
        cost_estimate=pl.CostEstimate(flops=10**10, bytes_accessed=12 << 20, transcendentals=0),
        name="upward",
    )(child, source, target, flat, m2m, far_op.reshape(1, CAP), near_op.reshape(1, PAIRS))


def serve_kernel(poles_ref, received_any, out_any, out_ref, ask_ref, in_sem, out_sem,
                 table_ref, stack_ref, place_ref, group_ref, hot_ref):
    asked = pltpu.make_async_copy(received_any.at[:, RANK:SENT, :], ask_ref, in_sem)
    asked.start()
    fill_table(table_ref)
    stack_groups(poles_ref, stack_ref)
    asked.wait()

    def unpack(n, _):
        for i in range(8):
            ask = ask_ref[n * 8 + i].astype(f32)
            place_ref[pl.ds(n * 8 + i, 1), :] = ask[0:1]
            group_ref[pl.ds(n * 8 + i, 1), :] = ask[1:2]
        return 0

    lax.fori_loop(0, PEERS // 8, unpack, 0)

    def store(d, block):
        out_ref[d, :, :] = block

    def flush(d):
        pltpu.make_async_copy(out_ref.at[pl.ds(d, FAR)], out_any.at[pl.ds(d, FAR)], out_sem).start()

    gather_rows(table_ref, stack_ref, place_ref, group_ref, hot_ref, store, flush)
    pltpu.make_async_copy(out_ref, out_any, out_sem).wait()


def serve(poles, received):
    return pl.pallas_call(
        serve_kernel,
        out_shape=jax.ShapeDtypeStruct((PEERS, RANK, CAP), bf16),
        in_specs=[VMEM, ANY],
        out_specs=ANY,
        scratch_shapes=[
            pltpu.VMEM((PEERS, RANK, CAP), bf16),
            pltpu.VMEM((PEERS, SENT - RANK, CAP), bf16),
            pltpu.SemaphoreType.DMA,
            pltpu.SemaphoreType.DMA,
        ] + GATHER_SCRATCH,
        compiler_params=pltpu.CompilerParams(vmem_limit_bytes=LIMIT),
        cost_estimate=pl.CostEstimate(flops=10**10, bytes_accessed=4 << 20, transcendentals=0),
        name="serve",
    )(poles, received)


def pick_lanes(poles_ref, lane, chunk, b):
    columns = []
    for t in range(TB // LANES):
        first = b * (TB // LANES) + t
        at = jnp.broadcast_to(lane[:, t * LANES:(t + 1) * LANES], (8, LANES)).astype(jnp.int32)
        where = jnp.broadcast_to(chunk[:, t * LANES:(t + 1) * LANES], (8, LANES))
        found = [jnp.zeros((8, LANES), f32)] * (RANK // 8)
        for k in range(first, BOX // LANES):
            mask = where == float(k)
            for r in range(RANK // 8):
                moved = jnp.take_along_axis(poles_ref[r * 8:(r + 1) * 8, k * LANES:(k + 1) * LANES], at, axis=1)
                found[r] = jnp.where(mask, moved, found[r])
        columns.append(jnp.concatenate(found, axis=0))
    return jnp.concatenate(columns, axis=1)


def near_kernel(first, batches, poles_ref, partner_ref, ops_ref, out_ref,
                table_ref, stack_ref, place_ref, group_ref, lane_ref, chunk_ref, poles32_ref, hot_ref, spread_ref,
                sum_ref, both_ref):
    fill_table(table_ref)
    poles32_ref[...] = poles_ref[...].astype(f32)
    stack_groups(poles_ref, stack_ref)
    for b in range(NB):
        for j in range(BATCH):
            partner = partner_ref[first + j * batches:first + (j + 1) * batches, b * TB:(b + 1) * TB]
            lanes = slice((b * BATCH + j) * TB, (b * BATCH + j + 1) * TB)
            place_ref[:, lanes], group_ref[:, lanes] = split_index(partner)
            if b >= BY_LANE:
                lane_ref[:, lanes] = (partner & (LANES - 1)).astype(f32)
                chunk_ref[:, lanes] = (partner >> 7).astype(f32)
    out_ref[...] = jnp.zeros(out_ref.shape, f32)

    def batch(n, _):
        ops = [take_op(ops_ref, first + j * batches + n, PAIRS) for j in range(BATCH)]
        ops = jnp.concatenate(ops + [jnp.transpose(op) for op in ops], axis=1)
        for b in range(NB):
            block = slice(b * TB, (b + 1) * TB)
            rows = (NB - b) * RANK
            for j in range(BATCH):
                lanes = slice((b * BATCH + j) * TB, (b * BATCH + j + 1) * TB)
                side = (b * BATCH + j) % SIDES
                place = place_ref[pl.ds(n, 1), lanes]
                group = group_ref[pl.ds(n, 1), lanes]
                hot_ref[side] = one_hot(table_ref, place)
                if b < BY_LANE:
                    found = jnp.dot(stack_ref[b * RANK:, :], hot_ref[side], preferred_element_type=f32)
                    both_ref[j * RANK:(j + 1) * RANK, block] = pick_group(found, group, b).astype(bf16)
                o = NB - 1 - b
                if o >= BY_LANE:
                    lanes = slice((o * BATCH + j) * TB, (o * BATCH + j + 1) * TB)
                    picked = pick_lanes(poles32_ref, lane_ref[pl.ds(n, 1), lanes], chunk_ref[pl.ds(n, 1), lanes], o)
                    both_ref[j * RANK:(j + 1) * RANK, o * TB:(o + 1) * TB] = picked.astype(bf16)
                spread_ref[side, :rows, :] = spread_group(poles_ref[:, block], group, b)
                added = lax.dot_general(spread_ref[side, :rows, :], hot_ref[side], NT, preferred_element_type=f32)
                if b > 0:
                    added += sum_ref[j, b * RANK:, :]
                done = WIDE + j * RANK
                both_ref[done:done + RANK, block] = added[0:RANK].astype(bf16)
                if b < NB - 1:
                    sum_ref[j, (b + 1) * RANK:, :] = added[RANK:]
        out_ref[...] += jnp.dot(ops, both_ref[...], preferred_element_type=f32)
        return 0

    lax.fori_loop(0, batches, batch, 0)


def near(poles, partner, ops, first, batches):
    return pl.pallas_call(
        functools.partial(near_kernel, first, batches),
        out_shape=jax.ShapeDtypeStruct((RANK, BOX), f32),
        in_specs=[VMEM] * 3,
        out_specs=VMEM,
        scratch_shapes=[
            pltpu.VMEM((TB, LANES), bf16),
            pltpu.VMEM((STACK, TB), bf16),
            pltpu.VMEM((batches, BATCH * BOX), f32),
            pltpu.VMEM((batches, BATCH * BOX), f32),
            pltpu.VMEM((batches, BATCH * BOX), f32),
            pltpu.VMEM((batches, BATCH * BOX), f32),
            pltpu.VMEM((RANK, BOX), f32),
            pltpu.VMEM((SIDES, TB, TB), bf16),
            pltpu.VMEM((SIDES, STACK, TB), bf16),
            pltpu.VMEM((BATCH, STACK, TB), f32),
            pltpu.VMEM((2 * WIDE, BOX), bf16),
        ],
        compiler_params=pltpu.CompilerParams(vmem_limit_bytes=LIMIT),
        cost_estimate=pl.CostEstimate(flops=10**9 * batches * BATCH, bytes_accessed=6 << 20, transcendentals=0),
        name="near",
    )(poles, partner, ops)


def down_kernel(served_any, own_any, near_a_ref, near_b_ref, source_ref, ops_ref, m2m_ref, out_any,
                served_ref, own_ref, out_ref, in_sem, out_sem,
                table_ref, place_ref, group_ref, hot_ref, spread_ref, total_ref, local_ref):
    def fetch(n):
        rows = pl.ds(n * FAR, FAR)
        return (pltpu.make_async_copy(served_any.at[rows], served_ref.at[rows], in_sem.at[0, n]),
                pltpu.make_async_copy(own_any.at[rows], own_ref.at[rows], in_sem.at[1, n]))

    for n in range(CAP // FAR):
        for copy in fetch(n):
            copy.start()
    fill_table(table_ref)
    place, group = split_index(source_ref[...])
    place_ref[...] = jnp.transpose(place)
    group_ref[...] = jnp.transpose(group)
    total_ref[...] = jnp.zeros(total_ref.shape, f32)

    def step(n, _):
        at = pl.multiple_of(n * FAR, FAR)
        for copy in fetch(n):
            copy.wait()
        source_places = place_ref[pl.ds(at, FAR), :]
        source_groups = group_ref[pl.ds(at, FAR), :]

        for i in range(0, FAR, 2):
            back, ahead, places, groups = [], [], [], []
            for k in range(2):
                c = at + i + k
                op = take_op(ops_ref, c, CAP)
                ahead.append(jnp.dot(op, served_ref[c], preferred_element_type=f32).astype(bf16))
                back.append(lax.dot_general(op, own_ref[c, 0:RANK, :], TN, preferred_element_type=f32).astype(bf16))
                ask = own_ref[c, RANK:SENT, :].astype(f32)
                places.append(ask[0:1])
                groups.append(ask[1:2])
            lanes = slice(2 * i * PEERS, (2 * i + 2) * PEERS)
            hot_ref[:, lanes] = one_hot(table_ref, side_by_side(source_places, i))
            spread_ref[:, lanes] = spread_group(jnp.concatenate(ahead, axis=1), side_by_side(source_groups, i))
            lanes = slice((2 * i + 2) * PEERS, (2 * i + 4) * PEERS)
            hot_ref[:, lanes] = one_hot(table_ref, jnp.concatenate(places, axis=1))
            spread_ref[:, lanes] = spread_group(jnp.concatenate(back, axis=1), jnp.concatenate(groups, axis=1))
        total_ref[...] += lax.dot_general(spread_ref[...], hot_ref[...], NT, preferred_element_type=f32)
        return 0

    lax.fori_loop(0, CAP // FAR, step, 0)
    ops = jnp.concatenate([m2m_ref[c] for c in range(CHILD)], axis=1)
    for k in range(NB):
        cols = slice(k * TB, (k + 1) * TB)
        far = total_ref[k * RANK:(k + 1) * RANK, :]
        local_ref[:, cols] = (near_a_ref[:, cols] + near_b_ref[:, cols] + far).astype(bf16)
        out_ref[:, cols] = lax.dot_general(
            ops, local_ref[:, cols], TN, preferred_element_type=f32).astype(bf16)
        if k % 4 == 3:
            cols = slice((k - 3) * TB, (k + 1) * TB)
            pltpu.make_async_copy(out_ref.at[:, cols], out_any.at[:, cols], out_sem).start()
    pltpu.make_async_copy(out_ref, out_any, out_sem).wait()


def downward(near_a, near_b, served, own, source, ops, m2m):
    return pl.pallas_call(
        down_kernel,
        out_shape=jax.ShapeDtypeStruct((CHILD * RANK, BOX), bf16),
        in_specs=[ANY] * 2 + [VMEM] * 5,
        out_specs=ANY,
        scratch_shapes=[
            pltpu.VMEM(served.shape, bf16),
            pltpu.VMEM(own.shape, bf16),
            pltpu.VMEM((CHILD * RANK, BOX), bf16),
            pltpu.SemaphoreType.DMA((2, CAP // FAR)),
            pltpu.SemaphoreType.DMA,
            pltpu.VMEM((TB, LANES), bf16),
            pltpu.VMEM((CAP, PEERS), f32),
            pltpu.VMEM((CAP, PEERS), f32),
            pltpu.VMEM((TB, 2 * FAR * PEERS), bf16),
            pltpu.VMEM((STACK, 2 * FAR * PEERS), bf16),
            pltpu.VMEM((STACK, TB), f32),
            pltpu.VMEM((RANK, BOX), bf16),
        ],
        compiler_params=pltpu.CompilerParams(vmem_limit_bytes=LIMIT),
        cost_estimate=pl.CostEstimate(flops=2 * 10**10, bytes_accessed=16 << 20, transcendentals=0),
        name="downward",
    )(served, own, near_a, near_b, source, ops, m2m)


def on_device(child_poles, m2m_ops, m2l_ops, near_partner, near_op, far_source, far_target, far_op):
    child = child_poles.reshape(CHILD * RANK, BOX)
    source = far_source[0]
    poles, send, far_ops, near_ops = upward(child, m2m_ops, source, far_target[0], far_op, near_op, m2l_ops)
    received = lax.all_to_all(send, ("curve", "sub"), split_axis=0, concat_axis=0, tiled=True)
    half = (PAIRS // BATCH + 1) // 2
    near_a = near(poles, near_partner, near_ops, 0, half)
    answer = serve(poles, received)
    fetched = lax.all_to_all(answer, ("curve", "sub"), split_axis=0, concat_axis=0, tiled=True)
    near_b = near(poles, near_partner, near_ops, half * BATCH, PAIRS // BATCH - half)
    own = jnp.transpose(received, (2, 1, 0))
    served = jnp.transpose(fetched, (2, 1, 0))
    out = downward(near_a, near_b, served, own, source, far_ops, m2m_ops)
    return out.reshape(CHILD, RANK, BOX)


def solution(mesh):
    placed = (
        P(None, None, ("curve", "sub")),
        P(),
        P(),
        P(None, ("curve", "sub")),
        P(),
        P(("curve", "sub"), None, None),
        P(("curve", "sub"), None, None),
        P(),
    )
    return jax.shard_map(
        on_device,
        mesh=mesh,
        in_specs=placed,
        out_specs=P(None, None, ("curve", "sub")),
        check_vma=False,
    )
```

```python
import functools

import jax
import jax.numpy as jnp
from jax import lax
from jax.experimental import pallas as pl
from jax.experimental.pallas import tpu as pltpu
from jax.sharding import PartitionSpec as P

RANK = 64
CHILD = 8
BOX = 2048
PEERS = 128
CAP = 128
PAIRS = 88
LANES = 128
TB = 256
NB = BOX // TB
STACK = NB * RANK
BATCH = 8
WIDE = BATCH * RANK
SIDES = 4
BY_LANE = 2
FAR = 8
EMPTY = 512
SENT = RANK + 16
f32 = jnp.float32
bf16 = jnp.bfloat16
VMEM = pl.BlockSpec(memory_space=pltpu.VMEM)
LIMIT = 56 * 2**20
ANY = pl.BlockSpec(memory_space=pl.ANY)
NT = (((1,), (1,)), ((), ()))
TN = (((0,), (0,)), ((), ()))


def fill_table(table_ref):
    table_ref[...] = lax.broadcasted_iota(jnp.int32, table_ref.shape, 0).astype(f32).astype(bf16)


def split_index(index):
    group = index >> 8
    place = jnp.where(index >= 0, index - group * TB, EMPTY)
    return place.astype(f32), jnp.maximum(group, 0).astype(f32)


def one_hot(table_ref, place):
    n = place.shape[1]
    row = jnp.broadcast_to(place, (16, n)).astype(bf16)
    parts = []
    for r in range(TB // 16):
        here = table_ref[r * 16:(r + 1) * 16, :]
        here = jnp.concatenate([here] * (n // LANES), axis=1)
        parts.append(jnp.where(here == row, jnp.ones((), bf16), jnp.zeros((), bf16)))
    return jnp.concatenate(parts, axis=0)


def pick_group(stacked, group, low=0):
    out = stacked[0:RANK]
    for k in range(low + 1, NB):
        out = jnp.where(group == float(k), stacked[(k - low) * RANK:(k - low + 1) * RANK], out)
    return out


def spread_group(values, group, low=0):
    n = values.shape[1]
    row = jnp.broadcast_to(group, (16, n)).astype(bf16)
    parts = []
    for k in range(low, NB):
        mask = row == jnp.array(k, bf16)
        parts += [jnp.where(mask, values[r * 16:(r + 1) * 16], jnp.zeros((), bf16)) for r in range(RANK // 16)]
    return jnp.concatenate(parts, axis=0)


def stack_groups(poles_ref, stack_ref):
    for k in range(NB):
        stack_ref[k * RANK:(k + 1) * RANK, :] = poles_ref[:, k * TB:(k + 1) * TB]


def side_by_side(rows, i):
    return jnp.concatenate([rows[i:i + 1], rows[i + 1:i + 2]], axis=1)


def gather_rows(table_ref, stack_ref, place_ref, group_ref, hot_ref, store, flush):
    def step(n, _):
        at = pl.multiple_of(n * FAR, FAR)
        places = place_ref[pl.ds(at, FAR), :]
        groups = group_ref[pl.ds(at, FAR), :]
        for i in range(0, FAR, 2):
            hot_ref[i // 2] = one_hot(table_ref, side_by_side(places, i))
            found = jnp.dot(stack_ref[...], hot_ref[i // 2], preferred_element_type=f32)
            found = pick_group(found, side_by_side(groups, i)).astype(bf16)
            store(at + i, found[:, :CAP])
            store(at + i + 1, found[:, CAP:])
        flush(at)
        return 0

    lax.fori_loop(0, PEERS // FAR, step, 0)


GATHER_SCRATCH = [
    pltpu.VMEM((TB, LANES), bf16),
    pltpu.VMEM((STACK, TB), bf16),
    pltpu.VMEM((PEERS, CAP), f32),
    pltpu.VMEM((PEERS, CAP), f32),
    pltpu.VMEM((FAR // 2, TB, 2 * CAP), bf16),
]


def select_ops(far_op_ref, near_op_ref, m2l_ref, ready, far_ref, near_ref):
    count = m2l_ref.shape[1]
    names = jnp.concatenate([far_op_ref[...], near_op_ref[...]], axis=1)
    hot = (lax.broadcasted_iota(jnp.int32, (count, CAP + PAIRS), 0) == names).astype(f32)
    hot = jnp.transpose(hot).astype(bf16)
    ready()
    for m in range(0, RANK // 2, 2):
        rows = [m2l_ref[r * RANK:(r + 1) * RANK, :] for r in (m, m + RANK // 2, m + 1, m + 1 + RANK // 2)]
        some = lax.dot_general(hot, jnp.concatenate(rows, axis=0), NT, preferred_element_type=f32)
        for i in range(2):
            pair = some[:, i * LANES:(i + 1) * LANES]
            far_ref[(m + i) * CAP:(m + i + 1) * CAP, :] = pair[:CAP]
            near_ref[(m + i) * PAIRS:(m + i + 1) * PAIRS, :] = pair[CAP:]


def take_op(ops_ref, s, slots):
    pairs = ops_ref[pl.ds(s, RANK // 2, stride=slots), :]
    return jnp.concatenate([pairs[:, :RANK], pairs[:, RANK:]], axis=0).astype(bf16)


def up_kernel(child_any, source_any, target_any, m2l_any, m2m_ref, far_op_ref, near_op_ref,
              poles_any, send_any, far_any, near_any,
              child_ref, source_ref, target_ref, m2l_ref, poles_ref, send_ref, far_ref, near_ref,
              in_sem, out_sem, ask_place_ref, ask_group_ref, table_ref, stack_ref, place_ref, group_ref, hot_ref):
    part = BOX // 4
    copies = [pltpu.make_async_copy(child_any.at[:, i * part:(i + 1) * part],
                                    child_ref.at[:, i * part:(i + 1) * part], in_sem.at[i]) for i in range(4)]
    copies += [pltpu.make_async_copy(source_any, source_ref, in_sem.at[4]),
               pltpu.make_async_copy(target_any, target_ref, in_sem.at[5]),
               pltpu.make_async_copy(m2l_any, m2l_ref, in_sem.at[6])]
    for copy in copies:
        copy.start()
    fill_table(table_ref)
    ops = jnp.concatenate([m2m_ref[c] for c in range(CHILD)], axis=1)
    for i in range(4):
        cols = slice(i * part, (i + 1) * part)
        copies[i].wait()
        poles_ref[:, cols] = jnp.dot(ops, child_ref[:, cols], preferred_element_type=f32).astype(bf16)
    poles_out = pltpu.make_async_copy(poles_ref, poles_any, out_sem.at[0])
    poles_out.start()
    stack_groups(poles_ref, stack_ref)
    copies[4].wait()
    copies[5].wait()
    place_ref[...], group_ref[...] = split_index(source_ref[...])
    ask_place_ref[...], ask_group_ref[...] = split_index(target_ref[...])
    sub = lax.broadcasted_iota(jnp.int32, (16, CAP), 0)

    def store(q, block):
        send_ref[q, 0:RANK, :] = block
        ask = jnp.where(sub == 0, ask_place_ref[pl.ds(q, 1), :],
                        jnp.where(sub == 1, ask_group_ref[pl.ds(q, 1), :], 0.0))
        send_ref[q, RANK:SENT, :] = ask.astype(bf16)

    def flush(q):
        pltpu.make_async_copy(send_ref.at[pl.ds(q, FAR)], send_any.at[pl.ds(q, FAR)], out_sem.at[1]).start()

    select_ops(far_op_ref, near_op_ref, m2l_ref, copies[6].wait, far_ref, near_ref)
    near_out = pltpu.make_async_copy(near_ref, near_any, out_sem.at[2])
    far_out = pltpu.make_async_copy(far_ref, far_any, out_sem.at[3])
    near_out.start()
    far_out.start()
    gather_rows(table_ref, stack_ref, place_ref, group_ref, hot_ref, store, flush)
    poles_out.wait()
    pltpu.make_async_copy(send_ref, send_any, out_sem.at[1]).wait()
    near_out.wait()
    far_out.wait()


def upward(child, m2m, source, target, far_op, near_op, m2l):
    flat = jnp.transpose(m2l, (1, 2, 0)).reshape(RANK * RANK, -1)
    out_shape = (
        jax.ShapeDtypeStruct((RANK, BOX), bf16),
        jax.ShapeDtypeStruct((PEERS, SENT, CAP), bf16),
        jax.ShapeDtypeStruct((RANK // 2 * CAP, LANES), f32),
        jax.ShapeDtypeStruct((RANK // 2 * PAIRS, LANES), f32),
    )
    return pl.pallas_call(
        up_kernel,
        out_shape=out_shape,
        in_specs=[ANY] * 4 + [VMEM] * 3,
        out_specs=(ANY,) * 4,
        scratch_shapes=[
            pltpu.VMEM(child.shape, bf16),
            pltpu.VMEM(source.shape, jnp.int32),
            pltpu.VMEM(target.shape, jnp.int32),
            pltpu.VMEM(flat.shape, bf16),
        ] + [pltpu.VMEM(o.shape, o.dtype) for o in out_shape] + [
            pltpu.SemaphoreType.DMA((7,)),
            pltpu.SemaphoreType.DMA((4,)),
            pltpu.VMEM((PEERS, CAP), f32),
            pltpu.VMEM((PEERS, CAP), f32),
        ] + GATHER_SCRATCH,
        compiler_params=pltpu.CompilerParams(vmem_limit_bytes=LIMIT),
        cost_estimate=pl.CostEstimate(flops=10**10, bytes_accessed=12 << 20, transcendentals=0),
        name="upward",
    )(child, source, target, flat, m2m, far_op.reshape(1, CAP), near_op.reshape(1, PAIRS))


def serve_kernel(poles_any, received_any, out_any, out_ref, ask_ref, in_sem, pole_sem, out_sem,
                 table_ref, stack_ref, place_ref, group_ref, hot_ref):
    asked = pltpu.make_async_copy(received_any.at[:, RANK:SENT, :], ask_ref, in_sem)
    asked.start()
    poles = [pltpu.make_async_copy(poles_any.at[:, k * TB:(k + 1) * TB],
                                   stack_ref.at[k * RANK:(k + 1) * RANK, :], pole_sem.at[k]) for k in range(NB)]
    for copy in poles:
        copy.start()
    fill_table(table_ref)
    for copy in poles:
        copy.wait()
    asked.wait()

    def unpack(n, _):
        for i in range(8):
            ask = ask_ref[n * 8 + i].astype(f32)
            place_ref[pl.ds(n * 8 + i, 1), :] = ask[0:1]
            group_ref[pl.ds(n * 8 + i, 1), :] = ask[1:2]
        return 0

    lax.fori_loop(0, PEERS // 8, unpack, 0)

    def store(d, block):
        out_ref[d, :, :] = block

    def flush(d):
        pltpu.make_async_copy(out_ref.at[pl.ds(d, FAR)], out_any.at[pl.ds(d, FAR)], out_sem).start()

    gather_rows(table_ref, stack_ref, place_ref, group_ref, hot_ref, store, flush)
    pltpu.make_async_copy(out_ref, out_any, out_sem).wait()


def serve(poles, received):
    return pl.pallas_call(
        serve_kernel,
        out_shape=jax.ShapeDtypeStruct((PEERS, RANK, CAP), bf16),
        in_specs=[ANY, ANY],
        out_specs=ANY,
        scratch_shapes=[
            pltpu.VMEM((PEERS, RANK, CAP), bf16),
            pltpu.VMEM((PEERS, SENT - RANK, CAP), bf16),
            pltpu.SemaphoreType.DMA,
            pltpu.SemaphoreType.DMA((NB,)),
            pltpu.SemaphoreType.DMA,
        ] + GATHER_SCRATCH,
        compiler_params=pltpu.CompilerParams(vmem_limit_bytes=LIMIT),
        cost_estimate=pl.CostEstimate(flops=10**10, bytes_accessed=4 << 20, transcendentals=0),
        name="serve",
    )(poles, received)


def pick_lanes(poles_ref, lane, chunk, b):
    columns = []
    for t in range(TB // LANES):
        first = b * (TB // LANES) + t
        at = jnp.broadcast_to(lane[:, t * LANES:(t + 1) * LANES], (8, LANES)).astype(jnp.int32)
        where = jnp.broadcast_to(chunk[:, t * LANES:(t + 1) * LANES], (8, LANES))
        found = [jnp.zeros((8, LANES), f32)] * (RANK // 8)
        for k in range(first, BOX // LANES):
            mask = where == float(k)
            for r in range(RANK // 8):
                moved = jnp.take_along_axis(poles_ref[r * 8:(r + 1) * 8, k * LANES:(k + 1) * LANES], at, axis=1)
                found[r] = jnp.where(mask, moved, found[r])
        columns.append(jnp.concatenate(found, axis=0))
    return jnp.concatenate(columns, axis=1)


def near_kernel(first, batches, poles_ref, partner_ref, ops_ref, out_ref,
                table_ref, stack_ref, place_ref, group_ref, lane_ref, chunk_ref, poles32_ref, hot_ref, spread_ref,
                sum_ref, both_ref):
    fill_table(table_ref)
    poles32_ref[...] = poles_ref[...].astype(f32)
    stack_groups(poles_ref, stack_ref)
    for b in range(NB):
        for j in range(BATCH):
            partner = partner_ref[first + j * batches:first + (j + 1) * batches, b * TB:(b + 1) * TB]
            lanes = slice((b * BATCH + j) * TB, (b * BATCH + j + 1) * TB)
            place_ref[:, lanes], group_ref[:, lanes] = split_index(partner)
            if b >= BY_LANE:
                lane_ref[:, lanes] = (partner & (LANES - 1)).astype(f32)
                chunk_ref[:, lanes] = (partner >> 7).astype(f32)
    out_ref[...] = jnp.zeros(out_ref.shape, f32)

    def batch(n, _):
        ops = [take_op(ops_ref, first + j * batches + n, PAIRS) for j in range(BATCH)]
        ops = jnp.concatenate(ops + [jnp.transpose(op) for op in ops], axis=1)
        for b in range(NB):
            block = slice(b * TB, (b + 1) * TB)
            rows = (NB - b) * RANK
            for j in range(BATCH):
                lanes = slice((b * BATCH + j) * TB, (b * BATCH + j + 1) * TB)
                side = (b * BATCH + j) % SIDES
                place = place_ref[pl.ds(n, 1), lanes]
                group = group_ref[pl.ds(n, 1), lanes]
                hot_ref[side] = one_hot(table_ref, place)
                if b < BY_LANE:
                    found = jnp.dot(stack_ref[b * RANK:, :], hot_ref[side], preferred_element_type=f32)
                    both_ref[j * RANK:(j + 1) * RANK, block] = pick_group(found, group, b).astype(bf16)
                o = NB - 1 - b
                if o >= BY_LANE:
                    lanes = slice((o * BATCH + j) * TB, (o * BATCH + j + 1) * TB)
                    picked = pick_lanes(poles32_ref, lane_ref[pl.ds(n, 1), lanes], chunk_ref[pl.ds(n, 1), lanes], o)
                    both_ref[j * RANK:(j + 1) * RANK, o * TB:(o + 1) * TB] = picked.astype(bf16)
                spread_ref[side, :rows, :] = spread_group(poles_ref[:, block], group, b)
                added = lax.dot_general(spread_ref[side, :rows, :], hot_ref[side], NT, preferred_element_type=f32)
                if b > 0:
                    added += sum_ref[j, b * RANK:, :]
                done = WIDE + j * RANK
                both_ref[done:done + RANK, block] = added[0:RANK].astype(bf16)
                if b < NB - 1:
                    sum_ref[j, (b + 1) * RANK:, :] = added[RANK:]
        out_ref[...] += jnp.dot(ops, both_ref[...], preferred_element_type=f32)
        return 0

    lax.fori_loop(0, batches, batch, 0)


def near(poles, partner, ops, first, batches):
    return pl.pallas_call(
        functools.partial(near_kernel, first, batches),
        out_shape=jax.ShapeDtypeStruct((RANK, BOX), f32),
        in_specs=[VMEM] * 3,
        out_specs=VMEM,
        scratch_shapes=[
            pltpu.VMEM((TB, LANES), bf16),
            pltpu.VMEM((STACK, TB), bf16),
            pltpu.VMEM((batches, BATCH * BOX), f32),
            pltpu.VMEM((batches, BATCH * BOX), f32),
            pltpu.VMEM((batches, BATCH * BOX), f32),
            pltpu.VMEM((batches, BATCH * BOX), f32),
            pltpu.VMEM((RANK, BOX), f32),
            pltpu.VMEM((SIDES, TB, TB), bf16),
            pltpu.VMEM((SIDES, STACK, TB), bf16),
            pltpu.VMEM((BATCH, STACK, TB), f32),
            pltpu.VMEM((2 * WIDE, BOX), bf16),
        ],
        compiler_params=pltpu.CompilerParams(vmem_limit_bytes=LIMIT),
        cost_estimate=pl.CostEstimate(flops=10**9 * batches * BATCH, bytes_accessed=6 << 20, transcendentals=0),
        name="near",
    )(poles, partner, ops)


def down_kernel(served_any, own_any, ops_any, near_a_any, near_b_any, source_ref, m2m_ref, out_any,
                served_ref, own_ref, ops_ref, near_a_ref, near_b_ref, out_ref, in_sem, more_sem, out_sem,
                table_ref, place_ref, group_ref, hot_ref, spread_ref, total_ref, local_ref):
    def fetch(n):
        rows = pl.ds(n * FAR, FAR)
        return (pltpu.make_async_copy(served_any.at[rows], served_ref.at[rows], in_sem.at[0, n]),
                pltpu.make_async_copy(own_any.at[rows], own_ref.at[rows], in_sem.at[1, n]))

    more = [pltpu.make_async_copy(a, b, more_sem.at[i]) for i, (a, b) in enumerate(
        ((ops_any, ops_ref), (near_a_any, near_a_ref), (near_b_any, near_b_ref)))]
    for copy in fetch(0) + tuple(more[:1]):
        copy.start()
    for n in range(1, CAP // FAR):
        for copy in fetch(n):
            copy.start()
    for copy in more[1:]:
        copy.start()
    fill_table(table_ref)
    place, group = split_index(source_ref[...])
    place_ref[...] = jnp.transpose(place)
    group_ref[...] = jnp.transpose(group)
    total_ref[...] = jnp.zeros(total_ref.shape, f32)

    def step(n, _):
        at = pl.multiple_of(n * FAR, FAR)
        for copy in fetch(n):
            copy.wait()
        source_places = place_ref[pl.ds(at, FAR), :]
        source_groups = group_ref[pl.ds(at, FAR), :]

        for i in range(0, FAR, 2):
            back, ahead, places, groups = [], [], [], []
            for k in range(2):
                c = at + i + k
                op = take_op(ops_ref, c, CAP)
                ahead.append(jnp.dot(op, served_ref[c], preferred_element_type=f32).astype(bf16))
                back.append(lax.dot_general(op, own_ref[c, 0:RANK, :], TN, preferred_element_type=f32).astype(bf16))
                ask = own_ref[c, RANK:SENT, :].astype(f32)
                places.append(ask[0:1])
                groups.append(ask[1:2])
            lanes = slice(2 * i * PEERS, (2 * i + 2) * PEERS)
            hot_ref[:, lanes] = one_hot(table_ref, side_by_side(source_places, i))
            spread_ref[:, lanes] = spread_group(jnp.concatenate(ahead, axis=1), side_by_side(source_groups, i))
            lanes = slice((2 * i + 2) * PEERS, (2 * i + 4) * PEERS)
            hot_ref[:, lanes] = one_hot(table_ref, jnp.concatenate(places, axis=1))
            spread_ref[:, lanes] = spread_group(jnp.concatenate(back, axis=1), jnp.concatenate(groups, axis=1))
        total_ref[...] += lax.dot_general(spread_ref[...], hot_ref[...], NT, preferred_element_type=f32)
        return 0

    more[0].wait()
    lax.fori_loop(0, CAP // FAR, step, 0)
    more[1].wait()
    more[2].wait()
    ops = jnp.concatenate([m2m_ref[c] for c in range(CHILD)], axis=1)
    for k in range(NB):
        cols = slice(k * TB, (k + 1) * TB)
        far = total_ref[k * RANK:(k + 1) * RANK, :]
        local_ref[:, cols] = (near_a_ref[:, cols] + near_b_ref[:, cols] + far).astype(bf16)
        out_ref[:, cols] = lax.dot_general(
            ops, local_ref[:, cols], TN, preferred_element_type=f32).astype(bf16)
        if k % 4 == 3:
            cols = slice((k - 3) * TB, (k + 1) * TB)
            pltpu.make_async_copy(out_ref.at[:, cols], out_any.at[:, cols], out_sem).start()
    pltpu.make_async_copy(out_ref, out_any, out_sem).wait()


def downward(near_a, near_b, served, own, source, ops, m2m):
    return pl.pallas_call(
        down_kernel,
        out_shape=jax.ShapeDtypeStruct((CHILD * RANK, BOX), bf16),
        in_specs=[ANY] * 5 + [VMEM] * 2,
        out_specs=ANY,
        scratch_shapes=[
            pltpu.VMEM(served.shape, bf16),
            pltpu.VMEM(own.shape, bf16),
            pltpu.VMEM(ops.shape, f32),
            pltpu.VMEM((RANK, BOX), f32),
            pltpu.VMEM((RANK, BOX), f32),
            pltpu.VMEM((CHILD * RANK, BOX), bf16),
            pltpu.SemaphoreType.DMA((2, CAP // FAR)),
            pltpu.SemaphoreType.DMA((3,)),
            pltpu.SemaphoreType.DMA,
            pltpu.VMEM((TB, LANES), bf16),
            pltpu.VMEM((CAP, PEERS), f32),
            pltpu.VMEM((CAP, PEERS), f32),
            pltpu.VMEM((TB, 2 * FAR * PEERS), bf16),
            pltpu.VMEM((STACK, 2 * FAR * PEERS), bf16),
            pltpu.VMEM((STACK, TB), f32),
            pltpu.VMEM((RANK, BOX), bf16),
        ],
        compiler_params=pltpu.CompilerParams(vmem_limit_bytes=LIMIT),
        cost_estimate=pl.CostEstimate(flops=2 * 10**10, bytes_accessed=16 << 20, transcendentals=0),
        name="downward",
    )(served, own, ops, near_a, near_b, source, m2m)


def on_device(child_poles, m2m_ops, m2l_ops, near_partner, near_op, far_source, far_target, far_op):
    child = child_poles.reshape(CHILD * RANK, BOX)
    source = far_source[0]
    poles, send, far_ops, near_ops = upward(child, m2m_ops, source, far_target[0], far_op, near_op, m2l_ops)
    received = lax.all_to_all(send, ("curve", "sub"), split_axis=0, concat_axis=0, tiled=True)
    half = (PAIRS // BATCH + 1) // 2
    near_a = near(poles, near_partner, near_ops, 0, half)
    answer = serve(poles, received)
    fetched = lax.all_to_all(answer, ("curve", "sub"), split_axis=0, concat_axis=0, tiled=True)
    near_b = near(poles, near_partner, near_ops, half * BATCH, PAIRS // BATCH - half)
    own = jnp.transpose(received, (2, 1, 0))
    served = jnp.transpose(fetched, (2, 1, 0))
    out = downward(near_a, near_b, served, own, source, far_ops, m2m_ops)
    return out.reshape(CHILD, RANK, BOX)


def solution(mesh):
    placed = (
        P(None, None, ("curve", "sub")),
        P(),
        P(),
        P(None, ("curve", "sub")),
        P(),
        P(("curve", "sub"), None, None),
        P(("curve", "sub"), None, None),
        P(),
    )
    return jax.shard_map(
        on_device,
        mesh=mesh,
        in_specs=placed,
        out_specs=P(None, None, ("curve", "sub")),
        check_vma=False,
    )
```

```python
import functools

import jax
import jax.numpy as jnp
from jax import lax
from jax.experimental import pallas as pl
from jax.experimental.pallas import tpu as pltpu
from jax.sharding import PartitionSpec as P

RANK = 64
CHILD = 8
BOX = 2048
PEERS = 128
CAP = 128
PAIRS = 88
LANES = 128
TB = 256
NB = BOX // TB
STACK = NB * RANK
BATCH = 8
WIDE = BATCH * RANK
SIDES = 4
BY_LANE = 2
FAR = 16
DOWN = 32
EMPTY = 512
SENT = RANK + 16
f32 = jnp.float32
bf16 = jnp.bfloat16
VMEM = pl.BlockSpec(memory_space=pltpu.VMEM)
LIMIT = 56 * 2**20
ANY = pl.BlockSpec(memory_space=pl.ANY)
NT = (((1,), (1,)), ((), ()))
TN = (((0,), (0,)), ((), ()))


def fill_table(table_ref):
    table_ref[...] = lax.broadcasted_iota(jnp.int32, table_ref.shape, 0).astype(f32).astype(bf16)


def split_index(index):
    group = index >> 8
    place = jnp.where(index >= 0, index - group * TB, EMPTY)
    return place.astype(f32), jnp.maximum(group, 0).astype(f32)


def one_hot(table_ref, place):
    n = place.shape[1]
    row = jnp.broadcast_to(place, (16, n)).astype(bf16)
    parts = []
    for r in range(TB // 16):
        here = table_ref[r * 16:(r + 1) * 16, :]
        here = jnp.concatenate([here] * (n // LANES), axis=1)
        parts.append(jnp.where(here == row, jnp.ones((), bf16), jnp.zeros((), bf16)))
    return jnp.concatenate(parts, axis=0)


def pick_group(stacked, group, low=0):
    out = stacked[0:RANK]
    for k in range(low + 1, NB):
        out = jnp.where(group == float(k), stacked[(k - low) * RANK:(k - low + 1) * RANK], out)
    return out


def spread_group(values, group, low=0):
    n = values.shape[1]
    row = jnp.broadcast_to(group, (16, n)).astype(bf16)
    parts = []
    for k in range(low, NB):
        mask = row == jnp.array(k, bf16)
        parts += [jnp.where(mask, values[r * 16:(r + 1) * 16], jnp.zeros((), bf16)) for r in range(RANK // 16)]
    return jnp.concatenate(parts, axis=0)


def stack_groups(poles_ref, stack_ref):
    for k in range(NB):
        stack_ref[k * RANK:(k + 1) * RANK, :] = poles_ref[:, k * TB:(k + 1) * TB]


def side_by_side(rows, i):
    return jnp.concatenate([rows[i:i + 1], rows[i + 1:i + 2]], axis=1)


def gather_rows(table_ref, stack_ref, place_ref, group_ref, hot_ref, store, flush):
    def step(n, _):
        at = pl.multiple_of(n * FAR, FAR)
        places = place_ref[pl.ds(at, FAR), :]
        groups = group_ref[pl.ds(at, FAR), :]
        for i in range(0, FAR, 2):
            hot_ref[i // 2] = one_hot(table_ref, side_by_side(places, i))
            found = jnp.dot(stack_ref[...], hot_ref[i // 2], preferred_element_type=f32)
            found = pick_group(found, side_by_side(groups, i)).astype(bf16)
            store(at + i, found[:, :CAP])
            store(at + i + 1, found[:, CAP:])
        flush(at)
        return 0

    lax.fori_loop(0, PEERS // FAR, step, 0)


GATHER_SCRATCH = [
    pltpu.VMEM((TB, LANES), bf16),
    pltpu.VMEM((STACK, TB), bf16),
    pltpu.VMEM((PEERS, CAP), f32),
    pltpu.VMEM((PEERS, CAP), f32),
    pltpu.VMEM((FAR // 2, TB, 2 * CAP), bf16),
]


def select_ops(far_op_ref, near_op_ref, m2l_ref, ready, far_ref, near_ref):
    count = m2l_ref.shape[1]
    names = jnp.concatenate([far_op_ref[...], near_op_ref[...]], axis=1)
    hot = (lax.broadcasted_iota(jnp.int32, (count, CAP + PAIRS), 0) == names).astype(f32)
    hot = jnp.transpose(hot).astype(bf16)
    ready()
    for m in range(0, RANK // 2, 2):
        rows = [m2l_ref[r * RANK:(r + 1) * RANK, :] for r in (m, m + RANK // 2, m + 1, m + 1 + RANK // 2)]
        some = lax.dot_general(hot, jnp.concatenate(rows, axis=0), NT, preferred_element_type=f32)
        for i in range(2):
            pair = some[:, i * LANES:(i + 1) * LANES]
            far_ref[(m + i) * CAP:(m + i + 1) * CAP, :] = pair[:CAP]
            near_ref[(m + i) * PAIRS:(m + i + 1) * PAIRS, :] = pair[CAP:]


def take_op(ops_ref, s, slots):
    pairs = ops_ref[pl.ds(s, RANK // 2, stride=slots), :]
    return jnp.concatenate([pairs[:, :RANK], pairs[:, RANK:]], axis=0).astype(bf16)


def up_kernel(child_any, source_any, target_any, m2l_any, m2m_ref, far_op_ref, near_op_ref,
              poles_any, send_any, far_any, near_any,
              child_ref, source_ref, target_ref, m2l_ref, poles_ref, send_ref, far_ref, near_ref,
              in_sem, out_sem, ask_place_ref, ask_group_ref, table_ref, stack_ref, place_ref, group_ref, hot_ref):
    part = BOX // 4
    copies = [pltpu.make_async_copy(child_any.at[:, i * part:(i + 1) * part],
                                    child_ref.at[:, i * part:(i + 1) * part], in_sem.at[i]) for i in range(4)]
    copies += [pltpu.make_async_copy(source_any, source_ref, in_sem.at[4]),
               pltpu.make_async_copy(target_any, target_ref, in_sem.at[5]),
               pltpu.make_async_copy(m2l_any, m2l_ref, in_sem.at[6])]
    for copy in copies:
        copy.start()
    fill_table(table_ref)
    ops = jnp.concatenate([m2m_ref[c] for c in range(CHILD)], axis=1)
    for i in range(4):
        cols = slice(i * part, (i + 1) * part)
        copies[i].wait()
        poles_ref[:, cols] = jnp.dot(ops, child_ref[:, cols], preferred_element_type=f32).astype(bf16)
    poles_out = pltpu.make_async_copy(poles_ref, poles_any, out_sem.at[0])
    poles_out.start()
    stack_groups(poles_ref, stack_ref)
    copies[4].wait()
    copies[5].wait()
    place_ref[...], group_ref[...] = split_index(source_ref[...])
    ask_place_ref[...], ask_group_ref[...] = split_index(target_ref[...])
    sub = lax.broadcasted_iota(jnp.int32, (16, CAP), 0)

    def store(q, block):
        send_ref[q, 0:RANK, :] = block
        ask = jnp.where(sub == 0, ask_place_ref[pl.ds(q, 1), :],
                        jnp.where(sub == 1, ask_group_ref[pl.ds(q, 1), :], 0.0))
        send_ref[q, RANK:SENT, :] = ask.astype(bf16)

    def flush(q):
        pltpu.make_async_copy(send_ref.at[pl.ds(q, FAR)], send_any.at[pl.ds(q, FAR)], out_sem.at[1]).start()

    select_ops(far_op_ref, near_op_ref, m2l_ref, copies[6].wait, far_ref, near_ref)
    near_out = pltpu.make_async_copy(near_ref, near_any, out_sem.at[2])
    far_out = pltpu.make_async_copy(far_ref, far_any, out_sem.at[3])
    near_out.start()
    far_out.start()
    gather_rows(table_ref, stack_ref, place_ref, group_ref, hot_ref, store, flush)
    poles_out.wait()
    pltpu.make_async_copy(send_ref, send_any, out_sem.at[1]).wait()
    near_out.wait()
    far_out.wait()


def upward(child, m2m, source, target, far_op, near_op, m2l):
    flat = jnp.transpose(m2l, (1, 2, 0)).reshape(RANK * RANK, -1)
    out_shape = (
        jax.ShapeDtypeStruct((RANK, BOX), bf16),
        jax.ShapeDtypeStruct((PEERS, SENT, CAP), bf16),
        jax.ShapeDtypeStruct((RANK // 2 * CAP, LANES), f32),
        jax.ShapeDtypeStruct((RANK // 2 * PAIRS, LANES), f32),
    )
    return pl.pallas_call(
        up_kernel,
        out_shape=out_shape,
        in_specs=[ANY] * 4 + [VMEM] * 3,
        out_specs=(ANY,) * 4,
        scratch_shapes=[
            pltpu.VMEM(child.shape, bf16),
            pltpu.VMEM(source.shape, jnp.int32),
            pltpu.VMEM(target.shape, jnp.int32),
            pltpu.VMEM(flat.shape, bf16),
        ] + [pltpu.VMEM(o.shape, o.dtype) for o in out_shape] + [
            pltpu.SemaphoreType.DMA((7,)),
            pltpu.SemaphoreType.DMA((4,)),
            pltpu.VMEM((PEERS, CAP), f32),
            pltpu.VMEM((PEERS, CAP), f32),
        ] + GATHER_SCRATCH,
        compiler_params=pltpu.CompilerParams(vmem_limit_bytes=LIMIT),
        cost_estimate=pl.CostEstimate(flops=10**10, bytes_accessed=12 << 20, transcendentals=0),
        name="upward",
    )(child, source, target, flat, m2m, far_op.reshape(1, CAP), near_op.reshape(1, PAIRS))


def serve_kernel(poles_any, received_any, out_any, out_ref, ask_ref, in_sem, pole_sem, out_sem,
                 table_ref, stack_ref, place_ref, group_ref, hot_ref):
    asked = pltpu.make_async_copy(received_any.at[:, RANK:SENT, :], ask_ref, in_sem)
    asked.start()
    poles = [pltpu.make_async_copy(poles_any.at[:, k * TB:(k + 1) * TB],
                                   stack_ref.at[k * RANK:(k + 1) * RANK, :], pole_sem.at[k]) for k in range(NB)]
    for copy in poles:
        copy.start()
    fill_table(table_ref)
    for copy in poles:
        copy.wait()
    asked.wait()

    def unpack(n, _):
        for i in range(8):
            ask = ask_ref[n * 8 + i].astype(f32)
            place_ref[pl.ds(n * 8 + i, 1), :] = ask[0:1]
            group_ref[pl.ds(n * 8 + i, 1), :] = ask[1:2]
        return 0

    lax.fori_loop(0, PEERS // 8, unpack, 0)

    def store(d, block):
        out_ref[d, :, :] = block

    def flush(d):
        pltpu.make_async_copy(out_ref.at[pl.ds(d, FAR)], out_any.at[pl.ds(d, FAR)], out_sem).start()

    gather_rows(table_ref, stack_ref, place_ref, group_ref, hot_ref, store, flush)
    pltpu.make_async_copy(out_ref, out_any, out_sem).wait()


def serve(poles, received):
    return pl.pallas_call(
        serve_kernel,
        out_shape=jax.ShapeDtypeStruct((PEERS, RANK, CAP), bf16),
        in_specs=[ANY, ANY],
        out_specs=ANY,
        scratch_shapes=[
            pltpu.VMEM((PEERS, RANK, CAP), bf16),
            pltpu.VMEM((PEERS, SENT - RANK, CAP), bf16),
            pltpu.SemaphoreType.DMA,
            pltpu.SemaphoreType.DMA((NB,)),
            pltpu.SemaphoreType.DMA,
        ] + GATHER_SCRATCH,
        compiler_params=pltpu.CompilerParams(vmem_limit_bytes=LIMIT),
        cost_estimate=pl.CostEstimate(flops=10**10, bytes_accessed=4 << 20, transcendentals=0),
        name="serve",
    )(poles, received)


def pick_lanes(poles_ref, lane, chunk, b):
    columns = []
    for t in range(TB // LANES):
        first = b * (TB // LANES) + t
        at = jnp.broadcast_to(lane[:, t * LANES:(t + 1) * LANES], (8, LANES)).astype(jnp.int32)
        where = jnp.broadcast_to(chunk[:, t * LANES:(t + 1) * LANES], (8, LANES))
        found = [jnp.zeros((8, LANES), f32)] * (RANK // 8)
        for k in range(first, BOX // LANES):
            mask = where == float(k)
            for r in range(RANK // 8):
                moved = jnp.take_along_axis(poles_ref[r * 8:(r + 1) * 8, k * LANES:(k + 1) * LANES], at, axis=1)
                found[r] = jnp.where(mask, moved, found[r])
        columns.append(jnp.concatenate(found, axis=0))
    return jnp.concatenate(columns, axis=1)


def near_kernel(first, batches, poles_ref, partner_ref, ops_ref, out_ref,
                table_ref, stack_ref, place_ref, group_ref, lane_ref, chunk_ref, poles32_ref, hot_ref, spread_ref,
                sum_ref, both_ref):
    fill_table(table_ref)
    poles32_ref[...] = poles_ref[...].astype(f32)
    stack_groups(poles_ref, stack_ref)
    for b in range(NB):
        for j in range(BATCH):
            partner = partner_ref[first + j * batches:first + (j + 1) * batches, b * TB:(b + 1) * TB]
            lanes = slice((b * BATCH + j) * TB, (b * BATCH + j + 1) * TB)
            place_ref[:, lanes], group_ref[:, lanes] = split_index(partner)
            if b >= BY_LANE:
                lane_ref[:, lanes] = (partner & (LANES - 1)).astype(f32)
                chunk_ref[:, lanes] = (partner >> 7).astype(f32)
    out_ref[...] = jnp.zeros(out_ref.shape, f32)

    def batch(n, _):
        ops = [take_op(ops_ref, first + j * batches + n, PAIRS) for j in range(BATCH)]
        ops = jnp.concatenate(ops + [jnp.transpose(op) for op in ops], axis=1)
        for b in range(NB):
            block = slice(b * TB, (b + 1) * TB)
            rows = (NB - b) * RANK
            for j in range(BATCH):
                lanes = slice((b * BATCH + j) * TB, (b * BATCH + j + 1) * TB)
                side = (b * BATCH + j) % SIDES
                place = place_ref[pl.ds(n, 1), lanes]
                group = group_ref[pl.ds(n, 1), lanes]
                hot_ref[side] = one_hot(table_ref, place)
                if b < BY_LANE:
                    found = jnp.dot(stack_ref[b * RANK:, :], hot_ref[side], preferred_element_type=f32)
                    both_ref[j * RANK:(j + 1) * RANK, block] = pick_group(found, group, b).astype(bf16)
                o = NB - 1 - b
                if o >= BY_LANE:
                    lanes = slice((o * BATCH + j) * TB, (o * BATCH + j + 1) * TB)
                    picked = pick_lanes(poles32_ref, lane_ref[pl.ds(n, 1), lanes], chunk_ref[pl.ds(n, 1), lanes], o)
                    both_ref[j * RANK:(j + 1) * RANK, o * TB:(o + 1) * TB] = picked.astype(bf16)
                spread_ref[side, :rows, :] = spread_group(poles_ref[:, block], group, b)
                added = lax.dot_general(spread_ref[side, :rows, :], hot_ref[side], NT, preferred_element_type=f32)
                if b > 0:
                    added += sum_ref[j, b * RANK:, :]
                done = WIDE + j * RANK
                both_ref[done:done + RANK, block] = added[0:RANK].astype(bf16)
                if b < NB - 1:
                    sum_ref[j, (b + 1) * RANK:, :] = added[RANK:]
        out_ref[...] += jnp.dot(ops, both_ref[...], preferred_element_type=f32)
        return 0

    lax.fori_loop(0, batches, batch, 0)


def near(poles, partner, ops, first, batches):
    return pl.pallas_call(
        functools.partial(near_kernel, first, batches),
        out_shape=jax.ShapeDtypeStruct((RANK, BOX), f32),
        in_specs=[VMEM] * 3,
        out_specs=VMEM,
        scratch_shapes=[
            pltpu.VMEM((TB, LANES), bf16),
            pltpu.VMEM((STACK, TB), bf16),
            pltpu.VMEM((batches, BATCH * BOX), f32),
            pltpu.VMEM((batches, BATCH * BOX), f32),
            pltpu.VMEM((batches, BATCH * BOX), f32),
            pltpu.VMEM((batches, BATCH * BOX), f32),
            pltpu.VMEM((RANK, BOX), f32),
            pltpu.VMEM((SIDES, TB, TB), bf16),
            pltpu.VMEM((SIDES, STACK, TB), bf16),
            pltpu.VMEM((BATCH, STACK, TB), f32),
            pltpu.VMEM((2 * WIDE, BOX), bf16),
        ],
        compiler_params=pltpu.CompilerParams(vmem_limit_bytes=LIMIT),
        cost_estimate=pl.CostEstimate(flops=10**9 * batches * BATCH, bytes_accessed=6 << 20, transcendentals=0),
        name="near",
    )(poles, partner, ops)


def down_kernel(served_any, own_any, near_a_ref, near_b_ref, source_ref, ops_ref, m2m_ref, out_any,
                served_ref, own_ref, out_ref, in_sem, out_sem,
                table_ref, place_ref, group_ref, hot_ref, spread_ref, total_ref, local_ref):
    def fetch(n):
        rows = pl.ds(n * DOWN, DOWN)
        return (pltpu.make_async_copy(served_any.at[rows], served_ref.at[rows], in_sem.at[0, n]),
                pltpu.make_async_copy(own_any.at[rows], own_ref.at[rows], in_sem.at[1, n]))

    for n in range(CAP // DOWN):
        for copy in fetch(n):
            copy.start()
    fill_table(table_ref)
    place, group = split_index(source_ref[...])
    place_ref[...] = jnp.transpose(place)
    group_ref[...] = jnp.transpose(group)
    total_ref[...] = jnp.zeros(total_ref.shape, f32)

    def step(n, _):
        at = pl.multiple_of(n * DOWN, DOWN)
        for copy in fetch(n):
            copy.wait()
        source_places = place_ref[pl.ds(at, DOWN), :]
        source_groups = group_ref[pl.ds(at, DOWN), :]

        for i in range(0, DOWN, 2):
            back, ahead, places, groups = [], [], [], []
            for k in range(2):
                c = at + i + k
                op = take_op(ops_ref, c, CAP)
                ahead.append(jnp.dot(op, served_ref[c], preferred_element_type=f32).astype(bf16))
                back.append(lax.dot_general(op, own_ref[c, 0:RANK, :], TN, preferred_element_type=f32).astype(bf16))
                ask = own_ref[c, RANK:SENT, :].astype(f32)
                places.append(ask[0:1])
                groups.append(ask[1:2])
            lanes = slice(2 * i * PEERS, (2 * i + 2) * PEERS)
            hot_ref[:, lanes] = one_hot(table_ref, side_by_side(source_places, i))
            spread_ref[:, lanes] = spread_group(jnp.concatenate(ahead, axis=1), side_by_side(source_groups, i))
            lanes = slice((2 * i + 2) * PEERS, (2 * i + 4) * PEERS)
            hot_ref[:, lanes] = one_hot(table_ref, jnp.concatenate(places, axis=1))
            spread_ref[:, lanes] = spread_group(jnp.concatenate(back, axis=1), jnp.concatenate(groups, axis=1))
        total_ref[...] += lax.dot_general(spread_ref[...], hot_ref[...], NT, preferred_element_type=f32)
        return 0

    lax.fori_loop(0, CAP // DOWN, step, 0)
    ops = jnp.concatenate([m2m_ref[c] for c in range(CHILD)], axis=1)
    for k in range(NB):
        cols = slice(k * TB, (k + 1) * TB)
        far = total_ref[k * RANK:(k + 1) * RANK, :]
        local_ref[:, cols] = (near_a_ref[:, cols] + near_b_ref[:, cols] + far).astype(bf16)
        out_ref[:, cols] = lax.dot_general(
            ops, local_ref[:, cols], TN, preferred_element_type=f32).astype(bf16)
        if k % 4 == 3:
            cols = slice((k - 3) * TB, (k + 1) * TB)
            pltpu.make_async_copy(out_ref.at[:, cols], out_any.at[:, cols], out_sem).start()
    pltpu.make_async_copy(out_ref, out_any, out_sem).wait()


def downward(near_a, near_b, served, own, source, ops, m2m):
    return pl.pallas_call(
        down_kernel,
        out_shape=jax.ShapeDtypeStruct((CHILD * RANK, BOX), bf16),
        in_specs=[ANY] * 2 + [VMEM] * 5,
        out_specs=ANY,
        scratch_shapes=[
            pltpu.VMEM(served.shape, bf16),
            pltpu.VMEM(own.shape, bf16),
            pltpu.VMEM((CHILD * RANK, BOX), bf16),
            pltpu.SemaphoreType.DMA((2, CAP // DOWN)),
            pltpu.SemaphoreType.DMA,
            pltpu.VMEM((TB, LANES), bf16),
            pltpu.VMEM((CAP, PEERS), f32),
            pltpu.VMEM((CAP, PEERS), f32),
            pltpu.VMEM((TB, 2 * DOWN * PEERS), bf16),
            pltpu.VMEM((STACK, 2 * DOWN * PEERS), bf16),
            pltpu.VMEM((STACK, TB), f32),
            pltpu.VMEM((RANK, BOX), bf16),
        ],
        compiler_params=pltpu.CompilerParams(vmem_limit_bytes=LIMIT),
        cost_estimate=pl.CostEstimate(flops=2 * 10**10, bytes_accessed=16 << 20, transcendentals=0),
        name="downward",
    )(served, own, near_a, near_b, source, ops, m2m)


def on_device(child_poles, m2m_ops, m2l_ops, near_partner, near_op, far_source, far_target, far_op):
    child = child_poles.reshape(CHILD * RANK, BOX)
    source = far_source[0]
    poles, send, far_ops, near_ops = upward(child, m2m_ops, source, far_target[0], far_op, near_op, m2l_ops)
    received = lax.all_to_all(send, ("curve", "sub"), split_axis=0, concat_axis=0, tiled=True)
    half = (PAIRS // BATCH + 1) // 2
    near_a = near(poles, near_partner, near_ops, 0, half)
    answer = serve(poles, received)
    fetched = lax.all_to_all(answer, ("curve", "sub"), split_axis=0, concat_axis=0, tiled=True)
    near_b = near(poles, near_partner, near_ops, half * BATCH, PAIRS // BATCH - half)
    own = jnp.transpose(received, (2, 1, 0))
    served = jnp.transpose(fetched, (2, 1, 0))
    out = downward(near_a, near_b, served, own, source, far_ops, m2m_ops)
    return out.reshape(CHILD, RANK, BOX)


def solution(mesh):
    placed = (
        P(None, None, ("curve", "sub")),
        P(),
        P(),
        P(None, ("curve", "sub")),
        P(),
        P(("curve", "sub"), None, None),
        P(("curve", "sub"), None, None),
        P(),
    )
    return jax.shard_map(
        on_device,
        mesh=mesh,
        in_specs=placed,
        out_specs=P(None, None, ("curve", "sub")),
        check_vma=False,
    )
```
